256 devices in a mesh: group: 4 (over y_hi, core), space: 64 (over y_lo, z, x).
Axes of the slice: x: 4, y: 4 (y_hi: 2, y_lo: 2; y = y_hi * 2 + y_lo), z: 8, core: 2. Of those that a mesh axis runs over, the one named last changes fastest.
Arguments:
- initial: float32 [512, 256, 128], P('space'), may hold values from -6 to 6
- source: float32 [512, 256, 128], P('space'), may hold values from -3 to 3
- table: float32 [8, 6], replicated, may hold values from 0 to 1
- pairs: int32 [4, 2], P('group'), may hold values from 0 to 7, as said below
- owner: int32 [256], replicated, may hold values from 0 to 255, each once
Outputs:
- mean: float32 [512, 256, 128], P(None, ('group', 'space'))
- variance: float32 [512, 256, 128], P(None, ('group', 'space'))
- first: float32 [6, 512, 256, 128], P(None, None, ('group', 'space'))
- total: float32 [6, 512, 256, 128], P(None, None, ('group', 'space'))
The draws below stay inside these ranges and needn't reach their ends.
Inputs may be any that keep to these rules, and one draw needn't show every extreme that they name: Every row of table appears exactly once in pairs. `owner`: every server slab position appears exactly once.
All inputs are finite; a program needn't handle non-finite values.
Results may differ from the reference program's by a relative error of at most 0.0003.
Values sent between devices are 32-bit elements; how exact they have to be, the bound alone decides.
No kernel may reach another device: no remote copies, remote signals or barrier semaphores. Data moves between devices by JAX's collectives and lax.ppermute only.
A program may use at most 128 MiB of HBM per device.

```python
import jax
import jax.numpy as jnp
from jax import lax

PARAMS = 6
GROUPS = 4
SAMPLES = 8
STEPS = 3
YS = 1
NZ = 128
SERVERS = 256
NX = 512
NY = 256


def draw_pairs(key, part):
    key = jax.random.fold_in(key, 11)
    order = jax.random.permutation(key, SAMPLES).astype(jnp.int32)
    return order.reshape(GROUPS, 2)


def shard_levels(key, extent, split, smallest, top_value):
    gain = 1.0
    for dim, parts in split:
        heights = jax.random.uniform(jax.random.fold_in(jax.random.fold_in(key, 6), dim), (parts,), jnp.float32, smallest / len(split), top_value / len(split))
        gain = gain * jnp.repeat(jnp.exp(heights), extent[dim] // parts).reshape((-1,) + (1,) * (len(extent) - 1 - dim))
    return gain


def normal_values(key, extent, deviation, limit, cuts=(), kind=jnp.bfloat16):
    drawn = jax.random.normal(key, extent, jnp.float32) * deviation
    if len(cuts) > 0:
        drawn = shard_levels(key, extent, cuts, -0.22, 0.18) * drawn
    return jnp.clip(drawn, min=-limit, max=limit).astype(kind)


def setup_inputs(seed: int = 0) -> dict:
    arg_keys = jax.random.split(jax.random.key(seed), 6)
    initial = normal_values(arg_keys[0], (NX, NY, NZ), 1.0, 6.0, ((0, 64),), jnp.float32)
    source = normal_values(arg_keys[1], (NX, NY, NZ), 0.5, 3.0, ((0, 64),), jnp.float32)
    table = jnp.clip(jax.random.uniform(arg_keys[2], (SAMPLES, PARAMS), jnp.float32, 0.0, 1.0), 0.0, 1.0)
    pairs = draw_pairs(jax.random.fold_in(arg_keys[5], 71), 0)
    owner = jax.random.permutation(arg_keys[4], SERVERS).astype(jnp.int32)
    return dict(initial=initial, source=source, table=table, pairs=pairs, owner=owner)


def run_params(table, pairs):
    labels = jnp.arange(table.shape[0], dtype=jnp.int32)
    pick_first = (pairs[:, 0][:, None] == labels[None, :]).astype(jnp.float32)
    pick_second = (pairs[:, 1][:, None] == labels[None, :]).astype(jnp.float32)
    first_draw = jnp.dot(pick_first, table, precision=lax.Precision.HIGHEST)
    second_draw = jnp.dot(pick_second, table, precision=lax.Precision.HIGHEST)
    frozen = jnp.eye(table.shape[1], dtype=jnp.int32) > 0
    mixed = jnp.where(frozen[None], second_draw[:, None, :], first_draw[:, None, :])
    return jnp.concatenate([first_draw[:, None], second_draw[:, None], mixed], axis=1)


def coefficients(unit):
    return (0.03 + 0.12 * unit[..., 0], 0.3 * unit[..., 1] - 0.15, 0.3 * unit[..., 2] - 0.15,
            0.3 * unit[..., 3] - 0.15, 0.02 + 0.2 * unit[..., 4], 0.5 + 1.5 * unit[..., 5])


def advance(extended, source, coeffs):
    diffusion, speed_x, speed_y, speed_z, decay, strength = coeffs
    inner = extended[..., 1:-1, :, :]
    widths = [(0, 0)] * (inner.ndim - 2) + [(1, 1), (1, 1)]
    padded = jnp.pad(inner, widths)
    east = extended[..., 2:, :, :]
    west = extended[..., :-2, :, :]
    north = padded[..., 2:, 1:-1]
    south = padded[..., :-2, 1:-1]
    upper = padded[..., 1:-1, 2:]
    lower = padded[..., 1:-1, :-2]
    laplace = east + west + north + south + upper + lower - 6.0 * inner
    transport = speed_x * (east - west) + speed_y * (north - south) + speed_z * (upper - lower)
    return inner + diffusion * laplace - 0.5 * transport - decay * inner + strength * source


def evolve(initial, source, unit):
    coeffs = coefficients(unit)
    field = initial
    for moment in range(STEPS):
        extended = jnp.pad(field, ((1, 1), (0, 0), (0, 0)))
        field = advance(extended, source, coeffs)
    return field


def reference(initial, source, table, pairs, owner):
    params = run_params(table, pairs)
    zero_field = jnp.zeros((NX, NY, NZ), jnp.float32)
    zero_stack = jnp.zeros((PARAMS, NX, NY, NZ), jnp.float32)

    def per_group(carry, unit_rows):
        sum_both, sum_square, sum_first, sum_total = carry
        snaps = lax.map(lambda unit: evolve(initial, source, unit), unit_rows)
        runs_a = snaps[0]
        runs_b = snaps[1]
        mixed_runs = snaps[2:]
        gap = runs_a[None] - mixed_runs
        sum_both = sum_both + runs_a + runs_b
        sum_square = sum_square + runs_a * runs_a + runs_b * runs_b
        sum_first = sum_first - runs_b[None] * gap
        sum_total = sum_total + gap * gap
        return (sum_both, sum_square, sum_first, sum_total), None

    sums, unused = lax.scan(per_group, (zero_field, zero_field, zero_stack, zero_stack), params)
    sum_both, sum_square, sum_first, sum_total = sums
    mean = sum_both / (2.0 * GROUPS)
    variance = sum_square / (2.0 * GROUPS) - mean * mean
    first = sum_first / (1.0 * GROUPS)
    total = sum_total / (2.0 * GROUPS)

    def to_servers(field):
        lead = field.shape[:-3]
        blocks = field.reshape(lead + (NX, SERVERS, YS, NZ))
        placed = jnp.zeros_like(blocks).at[..., owner, :, :].set(blocks)
        return placed.reshape(field.shape)

    return (to_servers(mean), to_servers(variance), to_servers(first), to_servers(total))
```

```python
import itertools

import jax
import jax.numpy as jnp
import numpy as np
from jax import lax
from jax.experimental import pallas as pl
from jax.experimental.pallas import tpu as pltpu
from jax.sharding import PartitionSpec as P


UROWS = 7
SROWS = 5
ROWS = UROWS + SROWS
PAIRS2 = list(itertools.combinations_with_replacement(range(4), 2))
PAIRS3 = list(itertools.combinations_with_replacement(range(4), 3))
FIELDS = 50
WIDE = 48
SECTION = WIDE * 8
DEPTH = 3 * SECTION + 128
ALPHA, KAPPA, HX, HY, HZ, STRENGTH, TWICE, SQUARE, ONE = range(9)


def terms():
    out = [(1.0, ALPHA, ALPHA, ALPHA)]
    out += [(3.0, ALPHA, ALPHA, 1 + i) for i in range(4)]
    for i, j in PAIRS2:
        many = 2.0 if i != j and i > 0 else 1.0
        out.append((3.0 * many, ALPHA, 1 + i, 1 + j))
    for i, j, k in PAIRS3:
        many = 1.0
        if i > 0:
            many = {1: 1.0, 2: 3.0, 3: 6.0}[len({i, j, k})]
        out.append((many, 1 + i, 1 + j, 1 + k))
    out.append((1.0, STRENGTH, SQUARE, ONE))
    out += [(1.0, STRENGTH, TWICE, 1 + i) for i in range(4)]
    for i, j in PAIRS2:
        many = 2.0 if i != j and i > 0 else 1.0
        out.append((many, STRENGTH, 1 + i, 1 + j))
    return out


def layout():
    listed = terms()
    factor = np.zeros((1, SECTION + 128), np.float32)
    which = np.full((3, SECTION + 128), ONE, np.int32)
    for column in range(SECTION + 128):
        if column < SECTION:
            feature = column // 8
        elif column < SECTION + 48:
            feature = WIDE + ((column - SECTION) // 8) % 2
        else:
            continue
        factor[0, column] = listed[feature][0]
        which[:, column] = listed[feature][1:]
    return factor, which


def pack_kernel(owner, place, initial, source, send, row, inverse):
    count = owner.shape[0]
    servers = send.shape[0]
    group, device = place[0], place[1]

    def invert(i, carry):
        inverse[owner[i]] = i
        return carry

    lax.fori_loop(0, count, invert, 0, unroll=8)
    row[0] = inverse[device]

    def fill(s, carry):
        p = inverse[group * servers + s]
        for array, rows, first in ((initial, UROWS, 0), (source, SROWS, UROWS)):
            for k in range(rows):
                y = p + k - rows // 2
                inside = jnp.logical_and(y >= 0, y < count)
                here = jnp.clip(y, 0, count - 1)
                value = array[pl.ds(here, 8, stride=count), :]
                send[s, first + k] = jnp.where(inside, value, 0.0)
        return carry

    lax.fori_loop(0, servers, fill, 0, unroll=2)


def shifted(value, lane):
    up = jnp.where(lane == 127, 0.0, pltpu.roll(value, 127, 1))
    down = jnp.where(lane == 0, 0.0, pltpu.roll(value, 1, 1))
    return up, down


def coefficients_into(table, pairs, factor, which, matrix):
    run = lax.broadcasted_iota(jnp.int32, (64, 128), 0) // 8
    same = (
        lax.broadcasted_iota(jnp.int32, (64, 128), 0) % 8
        == lax.broadcasted_iota(jnp.int32, (64, 128), 1) % 8
    )
    lane = lax.broadcasted_iota(jnp.int32, (64, 128), 1)
    for group in range(4):
        first, second = pairs[group, 0], pairs[group, 1]
        q = []
        for k in range(6):
            swap = jnp.logical_or(run == 1, run == 2 + k)
            q.append(jnp.where(swap, table[second, k], table[first, k]))
        kappa = 0.03 + 0.12 * q[0]
        hx, hy, hz = (-0.5 * (0.3 * q[1 + i] - 0.15) for i in range(3))
        decay = 0.02 + 0.2 * q[4]
        strength = 0.5 + 1.5 * q[5]
        alpha = 1.0 - 6.0 * kappa - decay
        values = [alpha, kappa, hx, hy, hz, strength, 2.0 * alpha + 1.0, alpha * alpha + alpha + 1.0]
        rows = slice(64 * group, 64 * group + 64)
        for chunk in range(SECTION // 128 + 1):
            columns = slice(128 * chunk, 128 * chunk + 128)
            product = jnp.broadcast_to(factor[:, columns], (64, 128))
            for part in range(3):
                index = jnp.broadcast_to(which[part : part + 1, columns], (64, 128))
                chosen = jnp.ones((64, 128), jnp.float32)
                for number, value in enumerate(values):
                    chosen = jnp.where(index == number, value, chosen)
                product = product * chosen
            split = product.reshape(8, 8, 128)
            split = jnp.concatenate([split[:2], split[2:] - split[:1]], axis=0)
            product = jnp.where(same, split.reshape(64, 128), 0.0)
            high = product.astype(jnp.bfloat16)
            low = (product - high.astype(jnp.float32)).astype(jnp.bfloat16)
            if chunk < SECTION // 128:
                matrix[rows, columns] = high
                matrix[rows, SECTION + 128 * chunk : SECTION + 128 * chunk + 128] = high
                matrix[rows, 2 * SECTION + 128 * chunk : 2 * SECTION + 128 * chunk + 128] = low
            else:
                tail = jnp.where(lane < 32, high.astype(jnp.float32), low.astype(jnp.float32))
                matrix[rows, 3 * SECTION :] = tail.astype(jnp.bfloat16)


def server_kernel(
    table, pairs, row, factor, which, received,
    mean, variance, first, total,
    u, s, f1, g1, f2, matrix, phi, result,
):
    blocks = 64
    p = row[0]
    lane = lax.broadcasted_iota(jnp.int32, (8, 128), 1)
    sub = lax.broadcasted_iota(jnp.int32, (8, 128), 0)
    keep = {k: jnp.where(jnp.logical_and(p + k >= 0, p + k < 256), 1.0, 0.0) for k in range(-2, 3)}

    def halo(ref, lead):
        ref[lead + (0,)] = jnp.where(sub == 0, 0.0, pltpu.roll(ref[lead + (blocks,)], 1, 0))
        ref[lead + (blocks + 1,)] = jnp.where(sub == 7, 0.0, pltpu.roll(ref[lead + (1,)], 7, 0))

    def copy(b, carry):
        start = (b // 8) * (ROWS * 8) + b % 8
        for k in range(ROWS):
            value = received[pl.ds(start + 8 * k, 8, stride=8 * ROWS * 8), :]
            if k < UROWS:
                u[k, b + 1] = value
            else:
                s[k - UROWS, b + 1] = value
        return carry

    lax.fori_loop(0, blocks, copy, 0, unroll=2)
    for k in range(UROWS):
        halo(u, (k,))
    for k in range(SROWS):
        halo(s, (k,))

    coefficients_into(table, pairs, factor, which, matrix)
    phi[...] = jnp.zeros(phi.shape, phi.dtype)

    def parts(ref, lead, k, b):
        c = ref[lead + (k, b + 1)]
        east, west = ref[lead + (k, b + 2)], ref[lead + (k, b)]
        north, south = ref[lead + (k + 1, b + 1)], ref[lead + (k - 1, b + 1)]
        up, down = shifted(c, lane)
        every = (east + west) + (north + south) + (up + down)
        return every, east - west, north - south, up - down

    def stage1(b, carry):
        for k in range(1, 6):
            out = parts(u, (), k, b)
            for i in range(4):
                value = out[i] if k == 3 else out[i] * keep[k - 3]
                f1[i, k - 1, b + 1] = value
        for k in range(1, 4):
            out = parts(s, (), k, b)
            for i in range(4):
                value = out[i] if k == 2 else out[i] * keep[k - 2]
                g1[i, k - 1, b + 1] = value
        return carry

    lax.fori_loop(0, blocks, stage1, 0)
    for i in range(4):
        for k in range(5):
            halo(f1, (i, k))
        for k in range(3):
            halo(g1, (i, k))

    def second(ref, k, b):
        a = [parts(ref, (i,), k, b) for i in range(4)]
        return [
            a[0][0],
            a[1][0] + a[0][1],
            a[2][0] + a[0][2],
            a[3][0] + a[0][3],
            a[1][1],
            a[2][1],
            a[3][1],
            a[2][2],
            a[3][2],
            a[3][3],
        ]

    def stage2(b, carry):
        for k in range(1, 4):
            for i, value in enumerate(second(f1, k, b)):
                f2[i, k - 1, b + 1] = value if k == 2 else value * keep[k - 2]
        return carry

    lax.fori_loop(0, blocks, stage2, 0)
    for i in range(10):
        for k in range(3):
            halo(f2, (i, k))

    def third(b):
        a = {pair: parts(f2, (i,), 1, b) for i, pair in enumerate(PAIRS2)}
        out = []
        for i, j, k in PAIRS3:
            if i > 0:
                value = a[(j, k)][i]
            elif j == 0 and k == 0:
                value = a[(0, 0)][0]
            elif j == 0:
                value = a[(0, k)][0] + a[(0, 0)][k]
            elif j == k:
                value = a[(j, j)][0] + a[(0, j)][j]
            else:
                value = 2.0 * a[(j, k)][0] + a[(0, k)][j] + a[(0, j)][k]
            out.append(value)
        return out

    def features(b):
        out = [u[3, b + 1]]
        out += [f1[i, 2, b + 1] for i in range(4)]
        out += [f2[i, 1, b + 1] for i in range(10)]
        out += third(b)
        out.append(s[2, b + 1])
        out += [g1[i, 1, b + 1] for i in range(4)]
        out += second(g1, 1, b)
        return out

    def stage3(pair, carry):
        for half in range(2):
            columns = slice(128 * half, 128 * half + 128)
            listed = features(2 * pair + half)
            for i in range(0, FIELDS, 2):
                value = jnp.concatenate([listed[i], listed[i + 1]], axis=0)
                high = value.astype(jnp.bfloat16)
                low = (value - high.astype(jnp.float32)).astype(jnp.bfloat16)
                if i < WIDE:
                    at = 8 * i
                    phi[at : at + 16, columns] = high
                    phi[SECTION + at : SECTION + at + 16, columns] = low
                    phi[2 * SECTION + at : 2 * SECTION + at + 16, columns] = high
                else:
                    at = 3 * SECTION
                    phi[at : at + 16, columns] = high
                    phi[at + 16 : at + 32, columns] = low
                    phi[at + 32 : at + 48, columns] = high
        result[...] = jnp.dot(matrix[...], phi[...], preferred_element_type=jnp.float32)
        for half in range(2):
            b = 2 * pair + half
            columns = slice(128 * half, 128 * half + 128)
            both = square = None
            firsts, totals = [None] * 6, [None] * 6

            def add(old, new):
                return new if old is None else old + new

            for group in range(4):
                base = 64 * group
                run_a = result[base : base + 8, columns]
                run_b = result[base + 8 : base + 16, columns]
                both = add(both, run_a + run_b)
                square = add(square, run_a * run_a + run_b * run_b)
                for i in range(6):
                    at = base + 16 + 8 * i
                    gap = result[at : at + 8, columns]
                    firsts[i] = add(firsts[i], run_b * gap)
                    totals[i] = add(totals[i], gap * gap)
            average = both * 0.125
            mean[pl.ds(b, 8, stride=64), :] = average
            variance[pl.ds(b, 8, stride=64), :] = square * 0.125 - average * average
            for i in range(6):
                first[pl.ds(512 * i + b, 8, stride=64), :] = firsts[i] * 0.25
                total[pl.ds(512 * i + b, 8, stride=64), :] = totals[i] * 0.125
        return carry

    lax.fori_loop(0, blocks // 2, stage3, 0)


def local(initial, source, table, pairs, owner):
    tile_x, rows_y, cells_z = initial.shape
    servers = lax.axis_size("space")
    group = lax.axis_index("group")
    place = jnp.stack([group, group * servers + lax.axis_index("space")]).astype(jnp.int32)
    all_pairs = lax.all_gather(pairs, "group", axis=0, tiled=True)
    smem = pl.BlockSpec(memory_space=pltpu.SMEM)
    vmem = pl.BlockSpec(memory_space=pltpu.VMEM)
    send, row = pl.pallas_call(
        pack_kernel,
        out_shape=(
            jax.ShapeDtypeStruct((servers, ROWS, 8, cells_z), jnp.float32),
            jax.ShapeDtypeStruct((1,), jnp.int32),
        ),
        in_specs=[smem, smem, vmem, vmem],
        out_specs=(vmem, smem),
        scratch_shapes=[pltpu.SMEM((rows_y,), jnp.int32)],
        compiler_params=pltpu.CompilerParams(vmem_limit_bytes=32 * 2**20),
    )(owner, place, initial.reshape(-1, cells_z), source.reshape(-1, cells_z))
    received = lax.all_to_all(send, "space", split_axis=0, concat_axis=0, tiled=True)
    factor, which = layout()
    cells_x = 8 * servers
    flat = jax.ShapeDtypeStruct((cells_x, cells_z), jnp.float32)
    six = jax.ShapeDtypeStruct((6 * cells_x, cells_z), jnp.float32)
    mean, variance, first, total = pl.pallas_call(
        server_kernel,
        out_shape=(flat, flat, six, six),
        in_specs=[smem, smem, smem, vmem, vmem, vmem],
        out_specs=(vmem,) * 4,
        scratch_shapes=[
            pltpu.VMEM((UROWS, 66, 8, 128), jnp.float32),
            pltpu.VMEM((SROWS, 66, 8, 128), jnp.float32),
            pltpu.VMEM((4, 5, 66, 8, 128), jnp.float32),
            pltpu.VMEM((4, 3, 66, 8, 128), jnp.float32),
            pltpu.VMEM((10, 3, 66, 8, 128), jnp.float32),
            pltpu.VMEM((256, DEPTH), jnp.bfloat16),
            pltpu.VMEM((DEPTH, 256), jnp.bfloat16),
            pltpu.VMEM((256, 256), jnp.float32),
        ],
        compiler_params=pltpu.CompilerParams(vmem_limit_bytes=56 * 2**20),
    )(table, all_pairs, row, jnp.asarray(factor), jnp.asarray(which), received.reshape(-1, cells_z))
    return (
        mean.reshape(cells_x, 1, cells_z),
        variance.reshape(cells_x, 1, cells_z),
        first.reshape(6, cells_x, 1, cells_z),
        total.reshape(6, cells_x, 1, cells_z),
    )


def solution(mesh):
    placed = (P("space", None, None), P("space", None, None), P(), P("group", None), P())
    return jax.shard_map(
        local,
        mesh=mesh,
        in_specs=placed,
        out_specs=(
            P(None, ("group", "space"), None),
            P(None, ("group", "space"), None),
            P(None, None, ("group", "space"), None),
            P(None, None, ("group", "space"), None),
        ),
        check_vma=False,
    )
```

```python
import itertools

import jax
import jax.numpy as jnp
import numpy as np
from jax import lax
from jax.experimental import pallas as pl
from jax.experimental.pallas import tpu as pltpu
from jax.sharding import PartitionSpec as P


NEAR_U, NEAR_S, FAR = 5, 3, 4
PAIRS2 = list(itertools.combinations_with_replacement(range(3), 2))
PAIRS3 = list(itertools.combinations_with_replacement(range(3), 3))
NEAR = 66
WIDE = 64
SECTION = WIDE * 8
DEPTH = 3 * SECTION + 128
COLUMNS = SECTION + 256
(ALPHA, KAPPA, HX, HZ, STRENGTH, UP, DOWN, UP2, DOWN2, U0, U0A, U1, UM1, S0, S0A, ONE) = range(16)
PAD = 8


def terms():
    word = (KAPPA, HX, HZ)

    def twice(i, j):
        return 2.0 if i != j and i > 0 else 1.0

    def thrice(i, j, k):
        return {1: 1.0, 2: 3.0, 3: 6.0}[len({i, j, k})] if i > 0 else 1.0

    out = [(1.0, U0, ONE, ONE)]
    out += [(1.0, U0A, w, ONE) for w in word]
    out += [(3.0 * twice(i, j), ALPHA, word[i], word[j]) for i, j in PAIRS2]
    out += [(thrice(i, j, k), word[i], word[j], word[k]) for i, j, k in PAIRS3]
    for whole, step in ((U1, UP), (UM1, DOWN)):
        out.append((1.0, whole, ONE, ONE))
        out += [(6.0, step, ALPHA, w) for w in word]
        out += [(3.0 * twice(i, j), step, word[i], word[j]) for i, j in PAIRS2]
    for square in (UP2, DOWN2):
        out.append((3.0, square, ALPHA, ONE))
        out += [(3.0, square, w, ONE) for w in word]
    out.append((1.0, S0, ONE, ONE))
    out += [(1.0, S0A, w, ONE) for w in word]
    out += [(twice(i, j), STRENGTH, word[i], word[j]) for i, j in PAIRS2]
    for step in (UP, DOWN):
        out.append((1.0, S0A, step, ONE))
        out += [(2.0, STRENGTH, step, w) for w in word]
    far = [(1.0, DOWN2, DOWN, ONE), (1.0, UP2, UP, ONE), (1.0, STRENGTH, DOWN2, ONE), (1.0, STRENGTH, UP2, ONE)]
    return out, far


def layout():
    near, far = terms()
    factor = np.zeros((1, COLUMNS), np.float32)
    which = np.full((3, COLUMNS), ONE, np.int32)
    for column in range(COLUMNS):
        if column < SECTION:
            term = near[column // 8]
        elif column < SECTION + 48:
            term = near[WIDE + (column - SECTION) // 8 % 2]
        elif SECTION + 128 <= column < SECTION + 224:
            term = far[(column - SECTION) // 8 % 4]
        else:
            continue
        factor[0, column] = term[0]
        which[:, column] = term[1:]
    return factor, which


def near_pack_kernel(owner, place, initial, source, send, row, padded_u, padded_s, inverse, sems):
    count = owner.shape[0]
    servers = send.shape[0]
    inner = pl.ds(PAD, count)
    copies = [
        pltpu.make_async_copy(initial, padded_u.at[:, inner, :], sems.at[0]),
        pltpu.make_async_copy(source, padded_s.at[:, inner, :], sems.at[1]),
    ]
    for copy in copies:
        copy.start()
    for ref in (padded_u, padded_s):
        for x in range(8):
            ref[x, :PAD] = jnp.zeros((PAD, 128), jnp.float32)
            ref[x, PAD + count :] = jnp.zeros((PAD, 128), jnp.float32)
    group, device = place[0], place[1]

    def invert(i, carry):
        inverse[owner[i]] = i
        return carry

    lax.fori_loop(0, count, invert, 0, unroll=8)
    row[0] = inverse[device]
    for copy in copies:
        copy.wait()
    first = lax.broadcasted_iota(jnp.int32, (8, 128), 0) < NEAR_U

    def fill(s, carry):
        p = inverse[group * servers + s] + PAD
        for x in range(8):
            rows_u = padded_u[x, pl.ds(p - NEAR_U // 2, 8), :]
            rows_s = padded_s[x, pl.ds(p - NEAR_S // 2 - NEAR_U, 8), :]
            send[s, x] = jnp.where(first, rows_u, rows_s)
        return carry

    lax.fori_loop(0, servers, fill, 0, unroll=2)


def far_pack_kernel(owner, place, initial, source, send, inverse):
    count = owner.shape[0]
    servers = send.shape[0]
    group = place[0]

    def invert(i, carry):
        inverse[owner[i]] = i
        return carry

    lax.fori_loop(0, count, invert, 0, unroll=8)

    def fill(s, carry):
        p = inverse[group * servers + s]
        for k, (array, step) in enumerate(((initial, -3), (initial, 3), (source, -2), (source, 2))):
            y = p + step
            inside = jnp.logical_and(y >= 0, y < count)
            value = array[pl.ds(jnp.clip(y, 0, count - 1), 8, stride=count), :]
            send[s, k] = jnp.where(inside, value, 0.0)
        return carry

    lax.fori_loop(0, servers, fill, 0, unroll=2)


def coefficient_kernel(rows_y, table, pairs, row, factor, which, near, far):
    p = row[0]
    run = lax.broadcasted_iota(jnp.int32, (64, 128), 0) // 8
    lane = lax.broadcasted_iota(jnp.int32, (64, 128), 1)
    same = lax.broadcasted_iota(jnp.int32, (64, 128), 0) % 8 == lane % 8

    def inside(k):
        return jnp.where(jnp.logical_and(p + k >= 0, p + k < rows_y), 1.0, 0.0)

    ways = inside(1) + inside(-1)
    ways_up = inside(2) + 1.0 + inside(-1)
    ways_down = inside(-2) + 1.0 + inside(1)
    for group in range(4):
        first, second = pairs[group, 0], pairs[group, 1]
        q = []
        for k in range(6):
            swap = jnp.logical_or(run == 1, run == 2 + k)
            q.append(jnp.where(swap, table[second, k], table[first, k]))
        kappa = 0.03 + 0.12 * q[0]
        hx, hy, hz = (-0.5 * (0.3 * q[1 + i] - 0.15) for i in range(3))
        decay = 0.02 + 0.2 * q[4]
        strength = 0.5 + 1.5 * q[5]
        alpha = 1.0 - 6.0 * kappa - decay
        up, down = kappa + hy, kappa - hy
        both = up * down
        values = [None] * ONE
        values[ALPHA], values[KAPPA], values[HX], values[HZ] = alpha, kappa, hx, hz
        values[STRENGTH], values[UP], values[DOWN] = strength, up, down
        values[UP2], values[DOWN2] = up * up, down * down
        values[U0] = alpha * (alpha * alpha + 3.0 * ways * both)
        values[U0A] = 3.0 * (alpha * alpha + ways * both)
        values[U1] = up * (3.0 * alpha * alpha + ways_up * both)
        values[UM1] = down * (3.0 * alpha * alpha + ways_down * both)
        values[S0] = strength * (alpha * alpha + alpha + 1.0 + ways * both)
        values[S0A] = strength * (2.0 * alpha + 1.0)
        rows = slice(64 * group, 64 * group + 64)
        for chunk in range(COLUMNS // 128):
            columns = slice(128 * chunk, 128 * chunk + 128)
            product = jnp.broadcast_to(factor[:, columns], (64, 128))
            for part in range(3):
                index = jnp.broadcast_to(which[part : part + 1, columns], (64, 128))
                chosen = jnp.ones((64, 128), jnp.float32)
                for number, value in enumerate(values):
                    chosen = jnp.where(index == number, value, chosen)
                product = product * chosen
            split = product.reshape(8, 8, 128)
            split = jnp.concatenate([split[:2], split[2:] - split[:1]], axis=0)
            product = jnp.where(same, split.reshape(64, 128), 0.0)
            high = product.astype(jnp.bfloat16)
            rest = product - high.astype(jnp.float32)
            if chunk < SECTION // 128:
                low = rest.astype(jnp.bfloat16)
                near[rows, columns] = high
                near[rows, SECTION + 128 * chunk : SECTION + 128 * chunk + 128] = high
                near[rows, 2 * SECTION + 128 * chunk : 2 * SECTION + 128 * chunk + 128] = low
            elif chunk == SECTION // 128:
                tail = jnp.where(lane < 32, high.astype(jnp.float32), rest)
                near[rows, 3 * SECTION :] = tail.astype(jnp.bfloat16)
            else:
                tail = jnp.where(lane < 64, high.astype(jnp.float32), rest)
                far[rows, :] = tail.astype(jnp.bfloat16)


def near_kernel(received, matrix, partial, rows, one, two, phi):
    blocks = partial.shape[0]
    size = 8 * blocks
    lane = lax.broadcasted_iota(jnp.int32, (8, 128), 1)
    zero = jnp.zeros((PAD, 128), jnp.float32)
    for ref, lead in ((rows, (8,)), (one, (3, 8)), (two, (6, 4))):
        for index in itertools.product(*(range(n) for n in lead)):
            ref[index + (slice(0, PAD),)] = zero
            ref[index + (slice(PAD + size, 2 * PAD + size),)] = zero
    phi[3 * SECTION :, :] = jnp.zeros((128, phi.shape[1]), phi.dtype)

    def at(b, step=0):
        return pl.ds(pl.multiple_of(8 * b, 8) + PAD + step, 8)

    def copy(b, carry):
        for k in range(8):
            rows[k, at(b), :] = received[pl.ds(64 * b + k, 8, stride=8), :]
        return carry

    lax.fori_loop(0, blocks, copy, 0, unroll=2)

    def parts(ref, lead, b):
        c = ref[lead + (at(b), slice(None))]
        east, west = ref[lead + (at(b, 1), slice(None))], ref[lead + (at(b, -1), slice(None))]
        up = jnp.where(lane == 127, 0.0, pltpu.roll(c, 127, 1))
        down = jnp.where(lane == 0, 0.0, pltpu.roll(c, 1, 1))
        return (east + west) + (up + down), east - west, up - down

    def stage1(b, carry):
        for k in range(8):
            for i, value in enumerate(parts(rows, (k,), b)):
                one[i, k, at(b), :] = value
        return carry

    lax.fori_loop(0, blocks, stage1, 0)
    inner = (1, 2, 3, 6)

    def stage2(b, carry):
        for n, k in enumerate(inner):
            m, x, z = (parts(one, (i, k), b) for i in range(3))
            words = (m[0], x[0] + m[1], z[0] + m[2], x[1], z[1], z[2])
            for i, value in enumerate(words):
                two[i, n, at(b), :] = value
        return carry

    lax.fori_loop(0, blocks, stage2, 0)

    def third(b):
        a = {pair: parts(two, (i, 1), b) for i, pair in enumerate(PAIRS2)}
        out = []
        for i, j, k in PAIRS3:
            if i > 0:
                value = a[(j, k)][i]
            elif j == 0 and k == 0:
                value = a[(0, 0)][0]
            elif j == 0:
                value = a[(0, k)][0] + a[(0, 0)][k]
            elif j == k:
                value = a[(j, j)][0] + a[(0, j)][j]
            else:
                value = 2.0 * a[(j, k)][0] + a[(0, k)][j] + a[(0, j)][k]
            out.append(value)
        return out

    def features(b):
        def words(k, n):
            out = [rows[k, at(b), :]] + [one[i, k, at(b), :] for i in range(3)]
            return out + [two[i, n, at(b), :] for i in range(6)] if n is not None else out

        out = words(2, 1) + third(b)
        out += words(3, 2) + words(1, 0)
        out += words(4, None) + words(0, None)
        out += words(6, 3) + words(7, None) + words(5, None)
        return out

    def stage3(pair, carry):
        for half in range(2):
            columns = slice(128 * half, 128 * half + 128)
            listed = features(2 * pair + half)
            for i in range(0, NEAR, 2):
                value = jnp.concatenate([listed[i], listed[i + 1]], axis=0)
                high = value.astype(jnp.bfloat16)
                low = (value - high.astype(jnp.float32)).astype(jnp.bfloat16)
                places = (8 * i, SECTION + 8 * i, 2 * SECTION + 8 * i)
                if i >= WIDE:
                    places = (3 * SECTION, 3 * SECTION + 16, 3 * SECTION + 32)
                for place, part in zip(places, (high, low, high)):
                    phi[place : place + 16, columns] = part
        result = jnp.dot(matrix[...], phi[...], preferred_element_type=jnp.float32)
        partial[2 * pair] = result[:, :128]
        partial[2 * pair + 1] = result[:, 128:]
        return carry

    lax.fori_loop(0, blocks // 2, stage3, 0)


def far_kernel(received, matrix, partial, mean, variance, first, total, phi, result):
    blocks = partial.shape[0]

    @pl.when(pl.program_id(0) == 0)
    def _():
        phi[96:, :] = jnp.zeros((32, phi.shape[1]), phi.dtype)

    for b in range(blocks):
        columns = slice(128 * b, 128 * b + 128)
        for i in range(0, FAR, 2):
            value = received[b, i : i + 2].reshape(16, 128)
            high = value.astype(jnp.bfloat16)
            low = (value - high.astype(jnp.float32)).astype(jnp.bfloat16)
            for place, part in zip((8 * i, 32 + 8 * i, 64 + 8 * i), (high, low, high)):
                phi[place : place + 16, columns] = part
    result[...] = jnp.dot(matrix[...], phi[...], preferred_element_type=jnp.float32)
    for b in range(blocks):
        columns = slice(128 * b, 128 * b + 128)
        out = slice(8 * b, 8 * b + 8)

        def run(number):
            rows = slice(8 * number, 8 * number + 8)
            return result[rows, columns] + partial[b, rows, :]

        def add(old, new):
            return new if old is None else old + new

        both = square = None
        firsts, totals = [None] * 6, [None] * 6
        for group in range(4):
            run_a, run_b = run(8 * group), run(8 * group + 1)
            both = add(both, run_a + run_b)
            square = add(square, run_a * run_a + run_b * run_b)
            for i in range(6):
                gap = run(8 * group + 2 + i)
                firsts[i] = add(firsts[i], run_b * gap)
                totals[i] = add(totals[i], gap * gap)
        average = both * 0.125
        mean[out, :] = average
        variance[out, :] = square * 0.125 - average * average
        for i in range(6):
            first[i, out, :] = firsts[i] * 0.25
            total[i, out, :] = totals[i] * 0.125


def shape(*dims):
    return jax.ShapeDtypeStruct(dims, jnp.float32)


def local(initial, source, table, pairs, owner):
    tile_x, rows_y, cells_z = initial.shape
    servers = lax.axis_size("space")
    group = lax.axis_index("group")
    place = jnp.stack([group, group * servers + lax.axis_index("space")]).astype(jnp.int32)
    all_pairs = lax.all_gather(pairs, "group", axis=0, tiled=True)
    smem = pl.BlockSpec(memory_space=pltpu.SMEM)
    vmem = pl.BlockSpec(memory_space=pltpu.VMEM)
    anywhere = pl.BlockSpec(memory_space=pl.ANY)
    limit = pltpu.CompilerParams(vmem_limit_bytes=32 * 2**20)
    near_send, row = pl.pallas_call(
        near_pack_kernel,
        out_shape=(shape(servers, 8, 8, cells_z), jax.ShapeDtypeStruct((1,), jnp.int32)),
        in_specs=[smem, smem, anywhere, anywhere],
        out_specs=(vmem, smem),
        scratch_shapes=[
            pltpu.VMEM((8, rows_y + 2 * PAD, cells_z), jnp.float32),
            pltpu.VMEM((8, rows_y + 2 * PAD, cells_z), jnp.float32),
            pltpu.SMEM((rows_y,), jnp.int32),
            pltpu.SemaphoreType.DMA((2,)),
        ],
        compiler_params=limit,
        name="near_pack",
    )(owner, place, initial, source)
    near_received = lax.all_to_all(near_send, "space", split_axis=0, concat_axis=0, tiled=True)
    far_send = pl.pallas_call(
        far_pack_kernel,
        out_shape=shape(servers, FAR, 8, cells_z),
        in_specs=[smem, smem, vmem, vmem],
        out_specs=vmem,
        scratch_shapes=[pltpu.SMEM((rows_y,), jnp.int32)],
        compiler_params=limit,
        name="far_pack",
    )(owner, place, initial.reshape(-1, cells_z), source.reshape(-1, cells_z))
    far_received = lax.all_to_all(far_send, "space", split_axis=0, concat_axis=0, tiled=True)
    factor, which = layout()

    def coefficients(*refs):
        coefficient_kernel(rows_y, *refs)

    near_matrix, far_matrix = pl.pallas_call(
        coefficients,
        out_shape=(
            jax.ShapeDtypeStruct((256, DEPTH), jnp.bfloat16),
            jax.ShapeDtypeStruct((256, 128), jnp.bfloat16),
        ),
        in_specs=[smem, smem, smem, vmem, vmem],
        out_specs=(vmem, vmem),
        compiler_params=limit,
        name="coefficients",
    )(table, all_pairs, row, jnp.asarray(factor), jnp.asarray(which))
    cells_x = 8 * servers
    long = cells_x + 2 * PAD
    partial = pl.pallas_call(
        near_kernel,
        out_shape=shape(servers, 256, cells_z),
        in_specs=[vmem, vmem],
        out_specs=vmem,
        scratch_shapes=[
            pltpu.VMEM((8, long, cells_z), jnp.float32),
            pltpu.VMEM((3, 8, long, cells_z), jnp.float32),
            pltpu.VMEM((6, 4, long, cells_z), jnp.float32),
            pltpu.VMEM((DEPTH, 256), jnp.bfloat16),
        ],
        compiler_params=pltpu.CompilerParams(vmem_limit_bytes=48 * 2**20),
        name="near",
    )(near_received.reshape(-1, cells_z), near_matrix)
    step = 4
    flat = pl.BlockSpec((8 * step, cells_z), lambda j: (j, 0))
    six = pl.BlockSpec((6, 8 * step, cells_z), lambda j: (0, j, 0))
    mean, variance, first, total = pl.pallas_call(
        far_kernel,
        grid=(servers // step,),
        out_shape=(shape(cells_x, cells_z), shape(cells_x, cells_z), shape(6, cells_x, cells_z), shape(6, cells_x, cells_z)),
        in_specs=[
            pl.BlockSpec((step, FAR, 8, cells_z), lambda j: (j, 0, 0, 0)),
            pl.BlockSpec((256, 128), lambda j: (0, 0)),
            pl.BlockSpec((step, 256, cells_z), lambda j: (j, 0, 0)),
        ],
        out_specs=(flat, flat, six, six),
        scratch_shapes=[
            pltpu.VMEM((128, 128 * step), jnp.bfloat16),
            pltpu.VMEM((256, 128 * step), jnp.float32),
        ],
        compiler_params=limit,
        name="far",
    )(far_received, far_matrix, partial)
    return (
        mean.reshape(cells_x, 1, cells_z),
        variance.reshape(cells_x, 1, cells_z),
        first.reshape(6, cells_x, 1, cells_z),
        total.reshape(6, cells_x, 1, cells_z),
    )


def solution(mesh):
    placed = (P("space", None, None), P("space", None, None), P(), P("group", None), P())
    return jax.shard_map(
        local,
        mesh=mesh,
        in_specs=placed,
        out_specs=(
            P(None, ("group", "space"), None),
            P(None, ("group", "space"), None),
            P(None, None, ("group", "space"), None),
            P(None, None, ("group", "space"), None),
        ),
        check_vma=False,
    )
```

```python
import itertools

import jax
import jax.numpy as jnp
import numpy as np
from jax import lax
from jax.experimental import pallas as pl
from jax.experimental.pallas import tpu as pltpu
from jax.sharding import Mesh, PartitionSpec as P


PAIRS2 = list(itertools.combinations_with_replacement(range(3), 2))
PAIRS3 = list(itertools.combinations_with_replacement(range(3), 3))
(ALPHA, KAPPA, HX, HZ, STRENGTH, UP, DOWN, UP2, DOWN2, U0, U0A, U1, UM1, S0, S0A, ONE) = range(16)
PAD = 8
GROUP = 4
U_WIDE, U_REST = 48, 2
S_WIDE, S_REST = 16, 4
U_DEPTH = 3 * 8 * U_WIDE + 128
S_DEPTH = 3 * 8 * S_WIDE + 128
AXES = {"yh": 2, "core": 2, "yl": 2, "z": 8, "x": 4}
SPACE = ("yl", "z", "x")
PLANE = ("yh", "core", "yl", "x")


def terms():
    word = (KAPPA, HX, HZ)

    def twice(i, j):
        return 2.0 if i != j and i > 0 else 1.0

    def thrice(i, j, k):
        return {1: 1.0, 2: 3.0, 3: 6.0}[len({i, j, k})] if i > 0 else 1.0

    u = [(1.0, U0, ONE, ONE)]
    u += [(1.0, U0A, w, ONE) for w in word]
    u += [(3.0 * twice(i, j), ALPHA, word[i], word[j]) for i, j in PAIRS2]
    u += [(thrice(i, j, k), word[i], word[j], word[k]) for i, j, k in PAIRS3]
    for whole, step in ((U1, UP), (UM1, DOWN)):
        u.append((1.0, whole, ONE, ONE))
        u += [(6.0, step, ALPHA, w) for w in word]
        u += [(3.0 * twice(i, j), step, word[i], word[j]) for i, j in PAIRS2]
    for square in (UP2, DOWN2):
        u.append((3.0, square, ALPHA, ONE))
        u += [(3.0, square, w, ONE) for w in word]
    u += [(1.0, UP2, UP, ONE), (1.0, DOWN2, DOWN, ONE)]
    s = [(1.0, S0, ONE, ONE)]
    s += [(1.0, S0A, w, ONE) for w in word]
    s += [(twice(i, j), STRENGTH, word[i], word[j]) for i, j in PAIRS2]
    for step in (UP, DOWN):
        s.append((1.0, S0A, step, ONE))
        s += [(2.0, STRENGTH, step, w) for w in word]
    s += [(1.0, STRENGTH, UP2, ONE), (1.0, STRENGTH, DOWN2, ONE)]
    return u, s


def layout():
    chosen = []
    for listed, wide, rest in zip(terms(), (U_WIDE, S_WIDE), (U_REST, S_REST)):
        chosen += [listed[c // 8] for c in range(8 * wide)]
        chosen += [listed[wide + c // 8 % rest] for c in range(24 * rest)]
        chosen += [(0.0, ONE, ONE, ONE)] * (128 - 24 * rest)
    factor = np.array([[term[0] for term in chosen]], np.float32)
    which = np.array([term[1:] for term in chosen], np.int32).T
    return factor, np.ascontiguousarray(which)


def pack_kernel(halo, owner, place, *refs):
    tiles, (send, row, padded, inverse, sems) = refs[:-5], refs[-5:]
    rows = 2 * halo + 1
    count = owner.shape[0]
    z, device = place[0], place[1]
    inner = pl.ds(PAD, count)
    slots = [(0, 2), (2, 2), (4, 2), (6, 2), (14, 2), (12, 2), (10, 2), (8, 1), (9, 1)]
    copies = []
    for n, (tile, (slot, many)) in enumerate(zip(tiles, slots)):
        copies.append(pltpu.make_async_copy(tile, padded.at[pl.ds(slot, many), inner, :], sems.at[n]))
    for copy in copies:
        copy.start()
    for i in range(16):
        padded[i, :PAD] = jnp.zeros((PAD, 128), jnp.float32)
        padded[i, PAD + count :] = jnp.zeros((PAD, 128), jnp.float32)

    def invert(i, carry):
        inverse[owner[i]] = i
        return carry

    lax.fori_loop(0, count, invert, 0, unroll=8)
    row[0] = inverse[device]
    for copy in copies:
        copy.wait()

    def fill(j, carry):
        target = (j // 8) * 64 + (j // 4 % 2) * 32 + z * 4 + j % 4
        start = inverse[target] + PAD - halo
        for i in range(16):
            send[j, rows * i : rows * i + rows, :] = padded[i, pl.ds(start, rows), :]
        return carry

    lax.fori_loop(0, send.shape[0], fill, 0, unroll=2)


def coefficient_kernel(rows_y, table, pairs, row, factor, which, u_matrix, s_matrix):
    p = row[0]
    run = lax.broadcasted_iota(jnp.int32, (64, 128), 0) // 8
    lane = lax.broadcasted_iota(jnp.int32, (64, 128), 1)
    same = lax.broadcasted_iota(jnp.int32, (64, 128), 0) % 8 == lane % 8

    def inside(k):
        return jnp.where(jnp.logical_and(p + k >= 0, p + k < rows_y), 1.0, 0.0)

    ways = inside(1) + inside(-1)
    ways_up = inside(2) + 1.0 + inside(-1)
    ways_down = inside(-2) + 1.0 + inside(1)
    for group in range(4):
        first, second = pairs[group, 0], pairs[group, 1]
        q = []
        for k in range(6):
            swap = jnp.logical_or(run == 1, run == 2 + k)
            q.append(jnp.where(swap, table[second, k], table[first, k]))
        kappa = 0.03 + 0.12 * q[0]
        hx, hy, hz = (-0.5 * (0.3 * q[1 + i] - 0.15) for i in range(3))
        decay = 0.02 + 0.2 * q[4]
        strength = 0.5 + 1.5 * q[5]
        alpha = 1.0 - 6.0 * kappa - decay
        up, down = kappa + hy, kappa - hy
        both = up * down
        values = [None] * ONE
        values[ALPHA], values[KAPPA], values[HX], values[HZ] = alpha, kappa, hx, hz
        values[STRENGTH], values[UP], values[DOWN] = strength, up, down
        values[UP2], values[DOWN2] = up * up, down * down
        values[U0] = alpha * (alpha * alpha + 3.0 * ways * both)
        values[U0A] = 3.0 * (alpha * alpha + ways * both)
        values[U1] = up * (3.0 * alpha * alpha + ways_up * both)
        values[UM1] = down * (3.0 * alpha * alpha + ways_down * both)
        values[S0] = strength * (alpha * alpha + alpha + 1.0 + ways * both)
        values[S0A] = strength * (2.0 * alpha + 1.0)
        rows = slice(64 * group, 64 * group + 64)
        chunk = 0
        for matrix, wide, rest in ((u_matrix, U_WIDE, U_REST), (s_matrix, S_WIDE, S_REST)):
            for at in range(0, 8 * wide + 128, 128):
                columns = slice(128 * chunk, 128 * chunk + 128)
                chunk += 1
                product = jnp.broadcast_to(factor[:, columns], (64, 128))
                for part in range(3):
                    index = jnp.broadcast_to(which[part : part + 1, columns], (64, 128))
                    chosen = jnp.ones((64, 128), jnp.float32)
                    for number, value in enumerate(values):
                        chosen = jnp.where(index == number, value, chosen)
                    product = product * chosen
                split = product.reshape(8, 8, 128)
                split = jnp.concatenate([split[:2], split[2:] - split[:1]], axis=0)
                product = jnp.where(same, split.reshape(64, 128), 0.0)
                high = product.astype(jnp.bfloat16)
                low = product - high.astype(jnp.float32)
                if at < 8 * wide:
                    matrix[rows, at : at + 128] = high
                    matrix[rows, 8 * wide + at : 8 * wide + at + 128] = high
                    matrix[rows, 16 * wide + at : 16 * wide + at + 128] = low.astype(jnp.bfloat16)
                else:
                    tail = jnp.where(lane < 16 * rest, high.astype(jnp.float32), low)
                    matrix[rows, 24 * wide :] = tail.astype(jnp.bfloat16)


def at(b, step=0):
    return pl.ds(pl.multiple_of(8 * b, 8) + PAD + step, 8)


def unpack(received, rows, z, blocks):
    many = rows.shape[0]
    device = 16 * many

    def copy(t, carry):
        r = (t // 4 % 8 - z + 8) % 8
        start = (t // 32 * 4 + t % 4) * device + 2 * many * r
        for x in range(2):
            for k in range(many):
                value = received[pl.ds(start + many * x + k, 4, stride=8 * device), :]
                rows.at[k][pl.ds(8 * t + PAD + x, 4, stride=2), :] = value
        return carry

    lax.fori_loop(0, blocks, copy, 0, unroll=2)


def clear_ends(size, *refs):
    zero = jnp.zeros((PAD, 128), jnp.float32)
    for ref in refs:
        for index in itertools.product(*(range(n) for n in ref.shape[:-2])):
            ref[index + (slice(0, PAD),)] = zero
            ref[index + (slice(PAD + size, 2 * PAD + size),)] = zero


def parts(ref, lead, b):
    lane = lax.broadcasted_iota(jnp.int32, (8, 128), 1)
    c = ref[lead + (at(b), slice(None))]
    east, west = ref[lead + (at(b, 1), slice(None))], ref[lead + (at(b, -1), slice(None))]
    up = jnp.where(lane == 127, 0.0, pltpu.roll(c, 127, 1))
    down = jnp.where(lane == 0, 0.0, pltpu.roll(c, 1, 1))
    return (east + west) + (up + down), east - west, up - down


def first_words(rows, one, skip, blocks):
    def body(b, carry):
        for n in range(one.shape[1]):
            for i, value in enumerate(parts(rows, (n + skip,), b)):
                one[i, n, at(b), :] = value
        return carry

    lax.fori_loop(0, blocks, body, 0)


def second_words(one, lead, b):
    m, x, z = (parts(one, (i, lead), b) for i in range(3))
    return [m[0], x[0] + m[1], z[0] + m[2], x[1], z[1], z[2]]


def third_words(two, lead, b):
    a = {pair: parts(two, (i, lead), b) for i, pair in enumerate(PAIRS2)}
    out = []
    for i, j, k in PAIRS3:
        if i > 0:
            value = a[(j, k)][i]
        elif j == 0 and k == 0:
            value = a[(0, 0)][0]
        elif j == 0:
            value = a[(0, k)][0] + a[(0, 0)][k]
        elif j == k:
            value = a[(j, j)][0] + a[(0, j)][j]
        else:
            value = 2.0 * a[(j, k)][0] + a[(0, k)][j] + a[(0, j)][k]
        out.append(value)
    return out


def store_features(phi, listed, wide, columns):
    rest = len(listed) - wide
    for i in range(0, len(listed), 2):
        value = jnp.concatenate([listed[i], listed[i + 1]], axis=0)
        high = value.astype(jnp.bfloat16)
        low = (value - high.astype(jnp.float32)).astype(jnp.bfloat16)
        base, size, here = (0, 8 * wide, i) if i < wide else (24 * wide, 8 * rest, i - wide)
        for n, part in enumerate((high, low, high)):
            place = base + size * n + 8 * here
            phi[place : place + 16, columns] = part


def u_kernel(place, received, matrix, partial, rows, one, two, phi):
    blocks = partial.shape[0]
    clear_ends(8 * blocks, rows, one, two)
    phi[24 * U_WIDE :, :] = jnp.zeros((128, phi.shape[1]), phi.dtype)
    unpack(received, rows, place[0], blocks)
    first_words(rows, one, 1, blocks)

    def second(b, carry):
        for n in range(3):
            for i, value in enumerate(second_words(one, n + 1, b)):
                two[i, n, at(b), :] = value
        return carry

    lax.fori_loop(0, blocks, second, 0)

    def words(k, b):
        out = [rows[k, at(b), :]]
        if 1 <= k <= 5:
            out += [one[i, k - 1, at(b), :] for i in range(3)]
        if 2 <= k <= 4:
            out += [two[i, k - 2, at(b), :] for i in range(6)]
        return out

    def last(group, carry):
        for n in range(GROUP):
            b = GROUP * group + n
            listed = words(3, b) + third_words(two, 1, b)
            for k in (4, 2, 5, 1, 6, 0):
                listed += words(k, b)
            store_features(phi, listed, U_WIDE, slice(128 * n, 128 * n + 128))
        result = jnp.dot(matrix[...], phi[...], preferred_element_type=jnp.float32)
        for n in range(GROUP):
            partial[GROUP * group + n] = result[:, 128 * n : 128 * n + 128]
        return carry

    lax.fori_loop(0, blocks // GROUP, last, 0)


def s_kernel(place, received, matrix, partial, mean, variance, first, total,
             rows, one, phi, result, mean_out, variance_out, first_out, total_out, sems):
    blocks = partial.shape[0]
    clear_ends(8 * blocks, rows, one)
    phi[24 * S_WIDE :, :] = jnp.zeros((128, phi.shape[1]), phi.dtype)
    unpack(received, rows, place[0], blocks)
    first_words(rows, one, 1, blocks)

    def add(old, new):
        return new if old is None else old + new

    def last(group, carry):
        for n in range(GROUP):
            b = GROUP * group + n

            def words(k):
                return [rows[k, at(b), :]] + [one[i, k - 1, at(b), :] for i in range(3)]

            listed = words(2) + second_words(one, 1, b) + words(3) + words(1)
            listed += [rows[4, at(b), :], rows[0, at(b), :]]
            store_features(phi, listed, S_WIDE, slice(128 * n, 128 * n + 128))
        result[...] = jnp.dot(matrix[...], phi[...], preferred_element_type=jnp.float32)
        for n in range(GROUP):
            b = GROUP * group + n
            columns = slice(128 * n, 128 * n + 128)
            out = pl.ds(pl.multiple_of(8 * b, 8), 8)

            def run(number):
                here = slice(8 * number, 8 * number + 8)
                return result[here, columns] + partial[b, here, :]

            both = square = None
            firsts, totals = [None] * 6, [None] * 6
            for g in range(4):
                run_a, run_b = run(8 * g), run(8 * g + 1)
                both = add(both, run_a + run_b)
                square = add(square, run_a * run_a + run_b * run_b)
                for i in range(6):
                    gap = run(8 * g + 2 + i)
                    firsts[i] = add(firsts[i], run_b * gap)
                    totals[i] = add(totals[i], gap * gap)
            average = both * 0.125
            mean_out[out, :] = average
            variance_out[out, :] = square * 0.125 - average * average
            for i in range(6):
                first_out[i, out, :] = firsts[i] * 0.25
                total_out[i, out, :] = totals[i] * 0.125
        return carry

    copies = []
    quarter = blocks // GROUP // 4
    for n in range(4):
        lax.fori_loop(n * quarter, n * quarter + quarter, last, 0)
        x = pl.ds(n * 2 * blocks, 2 * blocks)
        for k, (here, there) in enumerate(((mean_out, mean), (variance_out, variance))):
            copies.append(pltpu.make_async_copy(here.at[x, :], there.at[x, :], sems.at[4 * n + k]))
            copies[-1].start()
        for k, (here, there) in enumerate(((first_out, first), (total_out, total))):
            copies.append(pltpu.make_async_copy(here.at[:, x, :], there.at[:, x, :], sems.at[4 * n + 2 + k]))
            copies[-1].start()
    for copy in copies:
        copy.wait()


def shape(*dims):
    return jax.ShapeDtypeStruct(dims, jnp.float32)


def limit(mib):
    return pltpu.CompilerParams(vmem_limit_bytes=mib * 2**20)


def ring(tile):
    count = lax.axis_size("z")
    to_next = [(i, (i + 1) % count) for i in range(count)]
    to_last = [(i, (i - 1) % count) for i in range(count)]
    below, above = [tile], [tile]
    for _ in range(3):
        below.append(lax.ppermute(below[-1], "z", to_next))
        above.append(lax.ppermute(above[-1], "z", to_last))
    ends = [lax.ppermute(below[-1][:1], "z", to_next), lax.ppermute(above[-1][1:], "z", to_last)]
    return [tile] + above[1:] + below[1:] + ends


def local(initial, source, table, pairs, owner):
    tile_x, rows_y, cells_z = initial.shape
    servers = 64
    quarter = lax.axis_index(("yh", "core"))
    place = jnp.stack([lax.axis_index("z"), quarter * servers + lax.axis_index(SPACE)]).astype(jnp.int32)
    all_pairs = lax.all_gather(pairs, ("yh", "core"), axis=0, tiled=True)
    smem = pl.BlockSpec(memory_space=pltpu.SMEM)
    vmem = pl.BlockSpec(memory_space=pltpu.VMEM)
    anywhere = pl.BlockSpec(memory_space=pl.ANY)

    def deliver(array, halo, name):
        rows = 2 * halo + 1
        tiles = ring(lax.dynamic_slice_in_dim(array, 2 * quarter, 2, axis=0))
        send, row = pl.pallas_call(
            lambda *refs: pack_kernel(halo, *refs),
            out_shape=(shape(32, 16 * rows, cells_z), jax.ShapeDtypeStruct((1,), jnp.int32)),
            in_specs=[smem, smem] + [anywhere] * 9,
            out_specs=(vmem, smem),
            scratch_shapes=[
                pltpu.VMEM((16, rows_y + 2 * PAD, cells_z), jnp.float32),
                pltpu.SMEM((rows_y,), jnp.int32),
                pltpu.SemaphoreType.DMA((9,)),
            ],
            compiler_params=limit(8),
            name=name,
        )(owner, place, *tiles)
        received = lax.all_to_all(send, PLANE, split_axis=0, concat_axis=0, tiled=True)
        return received.reshape(-1, cells_z), row

    u_received, row = deliver(initial, 3, "u_pack")
    s_received, _ = deliver(source, 2, "s_pack")
    factor, which = layout()
    u_matrix, s_matrix = pl.pallas_call(
        lambda *refs: coefficient_kernel(rows_y, *refs),
        out_shape=(
            jax.ShapeDtypeStruct((256, U_DEPTH), jnp.bfloat16),
            jax.ShapeDtypeStruct((256, S_DEPTH), jnp.bfloat16),
        ),
        in_specs=[smem, smem, smem, vmem, vmem],
        out_specs=(vmem, vmem),
        compiler_params=limit(8),
        name="coefficients",
    )(table, all_pairs, row, jnp.asarray(factor), jnp.asarray(which))
    cells_x = tile_x * servers
    long = cells_x + 2 * PAD
    partial = pl.pallas_call(
        u_kernel,
        out_shape=shape(servers, 256, cells_z),
        in_specs=[smem, vmem, vmem],
        out_specs=vmem,
        scratch_shapes=[
            pltpu.VMEM((7, long, cells_z), jnp.float32),
            pltpu.VMEM((3, 5, long, cells_z), jnp.float32),
            pltpu.VMEM((6, 3, long, cells_z), jnp.float32),
            pltpu.VMEM((U_DEPTH, 128 * GROUP), jnp.bfloat16),
        ],
        compiler_params=limit(20),
        name="u_words",
    )(place, u_received, u_matrix)
    flat, six = shape(cells_x, cells_z), shape(6, cells_x, cells_z)
    mean, variance, first, total = pl.pallas_call(
        s_kernel,
        out_shape=(flat, flat, six, six),
        in_specs=[smem, vmem, vmem, vmem],
        out_specs=(anywhere,) * 4,
        scratch_shapes=[
            pltpu.VMEM((5, long, cells_z), jnp.float32),
            pltpu.VMEM((3, 3, long, cells_z), jnp.float32),
            pltpu.VMEM((S_DEPTH, 128 * GROUP), jnp.bfloat16),
            pltpu.VMEM((256, 128 * GROUP), jnp.float32),
            pltpu.VMEM(flat.shape, jnp.float32),
            pltpu.VMEM(flat.shape, jnp.float32),
            pltpu.VMEM(six.shape, jnp.float32),
            pltpu.VMEM(six.shape, jnp.float32),
            pltpu.SemaphoreType.DMA((16,)),
        ],
        compiler_params=limit(16),
        name="s_words",
    )(place, s_received, s_matrix, partial)
    return (
        mean.reshape(cells_x, 1, cells_z),
        variance.reshape(cells_x, 1, cells_z),
        first.reshape(6, cells_x, 1, cells_z),
        total.reshape(6, cells_x, 1, cells_z),
    )


def solution(mesh):
    axes = Mesh(mesh.devices.reshape(tuple(AXES.values())), tuple(AXES))
    group = ("yh", "core")
    placed = (P(SPACE, None, None), P(SPACE, None, None), P(), P(group, None), P())
    return jax.shard_map(
        local,
        mesh=axes,
        in_specs=placed,
        out_specs=(
            P(None, group + SPACE, None),
            P(None, group + SPACE, None),
            P(None, None, group + SPACE, None),
            P(None, None, group + SPACE, None),
        ),
        check_vma=False,
    )
```

```python
import itertools

import jax
import jax.numpy as jnp
import numpy as np
from jax import lax
from jax.experimental import pallas as pl
from jax.experimental.pallas import tpu as pltpu
from jax.sharding import PartitionSpec as P


NEAR_U, NEAR_S, FAR = 5, 3, 4
PAIRS2 = list(itertools.combinations_with_replacement(range(3), 2))
PAIRS3 = list(itertools.combinations_with_replacement(range(3), 3))
NEAR = 66
WIDE = 64
SECTION = WIDE * 8
DEPTH = 3 * SECTION + 128
COLUMNS = SECTION + 256
(ALPHA, KAPPA, HX, HZ, STRENGTH, UP, DOWN, UP2, DOWN2, U0, U0A, U1, UM1, S0, S0A, ONE) = range(16)
PAD = 8
GROUP = 4
DEEP = 4


def terms():
    word = (KAPPA, HX, HZ)

    def twice(i, j):
        return 2.0 if i != j and i > 0 else 1.0

    def thrice(i, j, k):
        return {1: 1.0, 2: 3.0, 3: 6.0}[len({i, j, k})] if i > 0 else 1.0

    out = [(1.0, U0, ONE, ONE)]
    out += [(1.0, U0A, w, ONE) for w in word]
    out += [(3.0 * twice(i, j), ALPHA, word[i], word[j]) for i, j in PAIRS2]
    out += [(thrice(i, j, k), word[i], word[j], word[k]) for i, j, k in PAIRS3]
    for whole, step in ((U1, UP), (UM1, DOWN)):
        out.append((1.0, whole, ONE, ONE))
        out += [(6.0, step, ALPHA, w) for w in word]
        out += [(3.0 * twice(i, j), step, word[i], word[j]) for i, j in PAIRS2]
    for square in (UP2, DOWN2):
        out.append((3.0, square, ALPHA, ONE))
        out += [(3.0, square, w, ONE) for w in word]
    out.append((1.0, S0, ONE, ONE))
    out += [(1.0, S0A, w, ONE) for w in word]
    out += [(twice(i, j), STRENGTH, word[i], word[j]) for i, j in PAIRS2]
    for step in (UP, DOWN):
        out.append((1.0, S0A, step, ONE))
        out += [(2.0, STRENGTH, step, w) for w in word]
    far = [(1.0, DOWN2, DOWN, ONE), (1.0, UP2, UP, ONE), (1.0, STRENGTH, DOWN2, ONE), (1.0, STRENGTH, UP2, ONE)]
    return out, far


def layout():
    near, far = terms()
    factor = np.zeros((1, COLUMNS), np.float32)
    which = np.full((3, COLUMNS), ONE, np.int32)
    for column in range(COLUMNS):
        if column < SECTION:
            term = near[column // 8]
        elif column < SECTION + 48:
            term = near[WIDE + (column - SECTION) // 8 % 2]
        elif SECTION + 128 <= column < SECTION + 224:
            term = far[(column - SECTION) // 8 % 4]
        else:
            continue
        factor[0, column] = term[0]
        which[:, column] = term[1:]
    return factor, which


def near_pack_kernel(place, owner_there, initial, source, send, padded_u, padded_s, ready, owner, inverse, sems):
    count = owner.shape[0]
    listed = pltpu.make_async_copy(owner_there, owner, sems.at[6])
    listed.start()
    servers = send.shape[0]
    inner = pl.ds(PAD, count)
    copies = [
        pltpu.make_async_copy(initial, padded_u.at[:, inner, :], sems.at[0]),
        pltpu.make_async_copy(source, padded_s.at[:, inner, :], sems.at[1]),
    ]
    for copy in copies:
        copy.start()
    for ref in (padded_u, padded_s):
        for x in range(8):
            ref[x, :PAD] = jnp.zeros((PAD, 128), jnp.float32)
            ref[x, PAD + count :] = jnp.zeros((PAD, 128), jnp.float32)
    group = place[0]
    listed.wait()

    def invert(i, carry):
        inverse[owner[i]] = i
        return carry

    lax.fori_loop(0, count, invert, 0, unroll=8)
    for copy in copies:
        copy.wait()
    first = lax.broadcasted_iota(jnp.int32, (8, 128), 0) < NEAR_U

    def fill(s, carry):
        p = inverse[group * servers + s] + PAD
        for x in range(8):
            rows_u = padded_u[x, pl.ds(p - NEAR_U // 2, 8), :]
            rows_s = padded_s[x, pl.ds(p - NEAR_S // 2 - NEAR_U, 8), :]
            ready[s, x] = jnp.where(first, rows_u, rows_s)
        return carry

    copies = []
    many = servers // 4
    for part in range(4):
        lax.fori_loop(part * many, part * many + many, fill, 0, unroll=2)
        here = pl.ds(part * many, many)
        copies.append(pltpu.make_async_copy(ready.at[here], send.at[here], sems.at[2 + part]))
        copies[-1].start()
    for copy in copies:
        copy.wait()


def far_pack_kernel(owner, place, initial, source, send, inverse):
    count = owner.shape[0]
    servers = send.shape[0]
    group = place[0]

    def invert(i, carry):
        inverse[owner[i]] = i
        return carry

    lax.fori_loop(0, count, invert, 0, unroll=8)

    def fill(s, carry):
        p = inverse[group * servers + s]
        for k, (array, step) in enumerate(((initial, -3), (initial, 3), (source, -2), (source, 2))):
            y = p + step
            inside = jnp.logical_and(y >= 0, y < count)
            value = array[pl.ds(jnp.clip(y, 0, count - 1), 8, stride=count), :]
            send[s, k] = jnp.where(inside, value, 0.0)
        return carry

    lax.fori_loop(0, servers, fill, 0, unroll=2)


def coefficient_kernel(table, pairs, owner, place, factor, which, near, far):
    rows_y = owner.shape[0]

    def find(i, found):
        return jnp.where(owner[i] == place[1], i, found)

    p = lax.fori_loop(0, rows_y, find, 0, unroll=8)
    run = lax.broadcasted_iota(jnp.int32, (64, 128), 0) // 8
    lane = lax.broadcasted_iota(jnp.int32, (64, 128), 1)
    same = lax.broadcasted_iota(jnp.int32, (64, 128), 0) % 8 == lane % 8

    def inside(k):
        return jnp.where(jnp.logical_and(p + k >= 0, p + k < rows_y), 1.0, 0.0)

    ways = inside(1) + inside(-1)
    ways_up = inside(2) + 1.0 + inside(-1)
    ways_down = inside(-2) + 1.0 + inside(1)
    for group in range(4):
        first, second = pairs[group, 0], pairs[group, 1]
        q = []
        for k in range(6):
            swap = jnp.logical_or(run == 1, run == 2 + k)
            q.append(jnp.where(swap, table[second, k], table[first, k]))
        kappa = 0.03 + 0.12 * q[0]
        hx, hy, hz = (-0.5 * (0.3 * q[1 + i] - 0.15) for i in range(3))
        decay = 0.02 + 0.2 * q[4]
        strength = 0.5 + 1.5 * q[5]
        alpha = 1.0 - 6.0 * kappa - decay
        up, down = kappa + hy, kappa - hy
        both = up * down
        values = [None] * ONE
        values[ALPHA], values[KAPPA], values[HX], values[HZ] = alpha, kappa, hx, hz
        values[STRENGTH], values[UP], values[DOWN] = strength, up, down
        values[UP2], values[DOWN2] = up * up, down * down
        values[U0] = alpha * (alpha * alpha + 3.0 * ways * both)
        values[U0A] = 3.0 * (alpha * alpha + ways * both)
        values[U1] = up * (3.0 * alpha * alpha + ways_up * both)
        values[UM1] = down * (3.0 * alpha * alpha + ways_down * both)
        values[S0] = strength * (alpha * alpha + alpha + 1.0 + ways * both)
        values[S0A] = strength * (2.0 * alpha + 1.0)
        rows = slice(64 * group, 64 * group + 64)
        for chunk in range(COLUMNS // 128):
            columns = slice(128 * chunk, 128 * chunk + 128)
            product = jnp.broadcast_to(factor[:, columns], (64, 128))
            for part in range(3):
                index = jnp.broadcast_to(which[part : part + 1, columns], (64, 128))
                chosen = jnp.ones((64, 128), jnp.float32)
                for number, value in enumerate(values):
                    chosen = jnp.where(index == number, value, chosen)
                product = product * chosen
            split = product.reshape(8, 8, 128)
            split = jnp.concatenate([split[:2], split[2:] - split[:1]], axis=0)
            product = jnp.where(same, split.reshape(64, 128), 0.0)
            high = product.astype(jnp.bfloat16)
            rest = product - high.astype(jnp.float32)
            if chunk < SECTION // 128:
                low = rest.astype(jnp.bfloat16)
                near[rows, columns] = high
                near[rows, SECTION + 128 * chunk : SECTION + 128 * chunk + 128] = high
                near[rows, 2 * SECTION + 128 * chunk : 2 * SECTION + 128 * chunk + 128] = low
            elif chunk == SECTION // 128:
                tail = jnp.where(lane < 32, high.astype(jnp.float32), rest)
                near[rows, 3 * SECTION :] = tail.astype(jnp.bfloat16)
            else:
                tail = jnp.where(lane < 64, high.astype(jnp.float32), rest)
                far[rows, :] = tail.astype(jnp.bfloat16)


def near_kernel(received, matrix, partial, rows, one, two, phi, ready, sems):
    blocks = partial.shape[0]
    size = 8 * blocks
    lane = lax.broadcasted_iota(jnp.int32, (8, 128), 1)
    zero = jnp.zeros((PAD, 128), jnp.float32)
    for ref, lead in ((rows, (8,)), (one, (3, 8)), (two, (6, 4))):
        for index in itertools.product(*(range(n) for n in lead)):
            ref[index + (slice(0, PAD),)] = zero
            ref[index + (slice(PAD + size, 2 * PAD + size),)] = zero
    phi[3 * SECTION :, :] = jnp.zeros((128, phi.shape[1]), phi.dtype)

    def at(b, step=0):
        return pl.ds(pl.multiple_of(8 * b, 8) + PAD + step, 8)

    def copy(b, carry):
        for k in range(8):
            rows[k, at(b), :] = received[pl.ds(64 * b + k, 8, stride=8), :]
        return carry

    lax.fori_loop(0, blocks, copy, 0, unroll=2)

    def parts(ref, lead, b):
        c = ref[lead + (at(b), slice(None))]
        east, west = ref[lead + (at(b, 1), slice(None))], ref[lead + (at(b, -1), slice(None))]
        up = jnp.where(lane == 127, 0.0, pltpu.roll(c, 127, 1))
        down = jnp.where(lane == 0, 0.0, pltpu.roll(c, 1, 1))
        return (east + west) + (up + down), east - west, up - down

    def stage1(b, carry):
        for k in range(8):
            for i, value in enumerate(parts(rows, (k,), b)):
                one[i, k, at(b), :] = value
        return carry

    lax.fori_loop(0, blocks, stage1, 0)
    inner = (1, 2, 3, 6)

    def stage2(b, carry):
        for n, k in enumerate(inner):
            m, x, z = (parts(one, (i, k), b) for i in range(3))
            words = (m[0], x[0] + m[1], z[0] + m[2], x[1], z[1], z[2])
            for i, value in enumerate(words):
                two[i, n, at(b), :] = value
        return carry

    lax.fori_loop(0, blocks, stage2, 0)

    def third(b):
        a = {pair: parts(two, (i, 1), b) for i, pair in enumerate(PAIRS2)}
        out = []
        for i, j, k in PAIRS3:
            if i > 0:
                value = a[(j, k)][i]
            elif j == 0 and k == 0:
                value = a[(0, 0)][0]
            elif j == 0:
                value = a[(0, k)][0] + a[(0, 0)][k]
            elif j == k:
                value = a[(j, j)][0] + a[(0, j)][j]
            else:
                value = 2.0 * a[(j, k)][0] + a[(0, k)][j] + a[(0, j)][k]
            out.append(value)
        return out

    def features(b):
        def words(k, n):
            out = [rows[k, at(b), :]] + [one[i, k, at(b), :] for i in range(3)]
            return out + [two[i, n, at(b), :] for i in range(6)] if n is not None else out

        out = words(2, 1) + third(b)
        out += words(3, 2) + words(1, 0)
        out += words(4, None) + words(0, None)
        out += words(6, 3) + words(7, None) + words(5, None)
        return out

    def sent(group, slot):
        here = partial.at[pl.ds(GROUP * group, GROUP)]
        return pltpu.make_async_copy(ready.at[slot], here, sems.at[slot])

    def stage3(group, carry):
        slot = group % 2

        @pl.when(group >= 2)
        def _():
            sent(group - 2, slot).wait()

        for n in range(GROUP):
            columns = slice(128 * n, 128 * n + 128)
            listed = features(GROUP * group + n)
            for i in range(0, NEAR, 2):
                value = jnp.concatenate([listed[i], listed[i + 1]], axis=0)
                high = value.astype(jnp.bfloat16)
                low = (value - high.astype(jnp.float32)).astype(jnp.bfloat16)
                places = (8 * i, SECTION + 8 * i, 2 * SECTION + 8 * i)
                if i >= WIDE:
                    places = (3 * SECTION, 3 * SECTION + 16, 3 * SECTION + 32)
                for place, part in zip(places, (high, low, high)):
                    phi[place : place + 16, columns] = part
        result = jnp.dot(matrix[...], phi[...], preferred_element_type=jnp.float32)
        for n in range(GROUP):
            ready[slot, n] = result[:, 128 * n : 128 * n + 128]
        sent(group, slot).start()
        return carry

    groups = blocks // GROUP
    lax.fori_loop(0, groups, stage3, 0)
    for group in (groups - 2, groups - 1):
        sent(group, group % 2).wait()


def far_kernel(received, matrix, partial, mean, variance, first, total,
               phi, result, near, mean_out, variance_out, first_out, total_out, near_sems, sems):
    blocks = partial.shape[0]
    groups = blocks // GROUP
    phi[96:, :] = jnp.zeros((32, phi.shape[1]), phi.dtype)

    def fetched(group, slot):
        return pltpu.make_async_copy(partial.at[pl.ds(GROUP * group, GROUP)], near.at[slot], near_sems.at[slot])

    for group in range(DEEP - 1):
        fetched(group, group).start()

    def add(old, new):
        return new if old is None else old + new

    def body(group, carry):
        slot = group % DEEP

        @pl.when(group + DEEP - 1 < groups)
        def _():
            fetched(group + DEEP - 1, (group + DEEP - 1) % DEEP).start()

        for n in range(GROUP):
            columns = slice(128 * n, 128 * n + 128)
            for i in range(0, FAR, 2):
                value = received[GROUP * group + n, i : i + 2].reshape(16, 128)
                high = value.astype(jnp.bfloat16)
                low = (value - high.astype(jnp.float32)).astype(jnp.bfloat16)
                for place, part in zip((8 * i, 32 + 8 * i, 64 + 8 * i), (high, low, high)):
                    phi[place : place + 16, columns] = part
        result[...] = jnp.dot(matrix[...], phi[...], preferred_element_type=jnp.float32)
        fetched(group, slot).wait()
        for n in range(GROUP):
            columns = slice(128 * n, 128 * n + 128)
            out = pl.ds(pl.multiple_of(8 * (GROUP * group + n), 8), 8)

            def run(number):
                rows = slice(8 * number, 8 * number + 8)
                return result[rows, columns] + near[slot, n, rows, :]

            both = square = None
            firsts, totals = [None] * 6, [None] * 6
            for g in range(4):
                run_a, run_b = run(8 * g), run(8 * g + 1)
                both = add(both, run_a + run_b)
                square = add(square, run_a * run_a + run_b * run_b)
                for i in range(6):
                    gap = run(8 * g + 2 + i)
                    firsts[i] = add(firsts[i], run_b * gap)
                    totals[i] = add(totals[i], gap * gap)
            average = both * 0.125
            mean_out[out, :] = average
            variance_out[out, :] = square * 0.125 - average * average
            for i in range(6):
                first_out[i, out, :] = firsts[i] * 0.25
                total_out[i, out, :] = totals[i] * 0.125
        return carry

    copies = []
    quarter = groups // 4
    size = 2 * blocks
    for n in range(4):
        lax.fori_loop(n * quarter, n * quarter + quarter, body, 0)
        x = pl.ds(n * size, size)
        for k, (here, there) in enumerate(((mean_out, mean), (variance_out, variance))):
            copies.append(pltpu.make_async_copy(here.at[x, :], there.at[x, :], sems.at[4 * n + k]))
            copies[-1].start()
        for k, (here, there) in enumerate(((first_out, first), (total_out, total))):
            copies.append(pltpu.make_async_copy(here.at[:, x, :], there.at[:, x, :], sems.at[4 * n + 2 + k]))
            copies[-1].start()
    for copy in copies:
        copy.wait()


def shape(*dims):
    return jax.ShapeDtypeStruct(dims, jnp.float32)


def held(array):
    return pltpu.with_memory_space_constraint(array, pltpu.HBM)


def limit(mib):
    return pltpu.CompilerParams(vmem_limit_bytes=mib * 2**20)


def local(initial, source, table, pairs, owner):
    tile_x, rows_y, cells_z = initial.shape
    servers = lax.axis_size("space")
    group = lax.axis_index("group")
    place = jnp.stack([group, group * servers + lax.axis_index("space")]).astype(jnp.int32)
    all_pairs = lax.all_gather(pairs, "group", axis=0, tiled=True)
    smem = pl.BlockSpec(memory_space=pltpu.SMEM)
    vmem = pl.BlockSpec(memory_space=pltpu.VMEM)
    hbm = pl.BlockSpec(memory_space=pltpu.HBM)
    near_send = pl.pallas_call(
        near_pack_kernel,
        out_shape=pltpu.HBM((servers, 8, 8, cells_z), jnp.float32),
        in_specs=[smem, hbm, hbm, hbm],
        out_specs=hbm,
        scratch_shapes=[
            pltpu.VMEM((8, rows_y + 2 * PAD, cells_z), jnp.float32),
            pltpu.VMEM((8, rows_y + 2 * PAD, cells_z), jnp.float32),
            pltpu.VMEM((servers, 8, 8, cells_z), jnp.float32),
            pltpu.SMEM((rows_y,), jnp.int32),
            pltpu.SMEM((rows_y,), jnp.int32),
            pltpu.SemaphoreType.DMA((7,)),
        ],
        compiler_params=limit(8),
        name="near_pack",
    )(place, held(owner), held(initial), held(source))
    near_received = lax.all_to_all(near_send, "space", split_axis=0, concat_axis=0, tiled=True)
    far_send = pl.pallas_call(
        far_pack_kernel,
        out_shape=shape(servers, FAR, 8, cells_z),
        in_specs=[smem, smem, vmem, vmem],
        out_specs=vmem,
        scratch_shapes=[pltpu.SMEM((rows_y,), jnp.int32)],
        compiler_params=limit(8),
        name="far_pack",
    )(owner, place, initial.reshape(-1, cells_z), source.reshape(-1, cells_z))
    factor, which = layout()
    near_matrix, far_matrix = pl.pallas_call(
        coefficient_kernel,
        out_shape=(
            jax.ShapeDtypeStruct((256, DEPTH), jnp.bfloat16),
            jax.ShapeDtypeStruct((256, 128), jnp.bfloat16),
        ),
        in_specs=[smem, smem, smem, smem, vmem, vmem],
        out_specs=(vmem, vmem),
        compiler_params=limit(8),
        name="coefficients",
    )(table, all_pairs, owner, place, jnp.asarray(factor), jnp.asarray(which))
    far_send, near_matrix, far_matrix = lax.optimization_barrier((far_send, near_matrix, far_matrix))
    far_received = lax.all_to_all(far_send, "space", split_axis=0, concat_axis=0, tiled=True)
    cells_x = 8 * servers
    long = cells_x + 2 * PAD
    partial = pl.pallas_call(
        near_kernel,
        out_shape=pltpu.HBM((servers, 256, cells_z), jnp.float32),
        in_specs=[vmem, vmem],
        out_specs=hbm,
        scratch_shapes=[
            pltpu.VMEM((8, long, cells_z), jnp.float32),
            pltpu.VMEM((3, 8, long, cells_z), jnp.float32),
            pltpu.VMEM((6, 4, long, cells_z), jnp.float32),
            pltpu.VMEM((DEPTH, 128 * GROUP), jnp.bfloat16),
            pltpu.VMEM((2, GROUP, 256, cells_z), jnp.float32),
            pltpu.SemaphoreType.DMA((2,)),
        ],
        compiler_params=limit(24),
        name="near",
    )(near_received.reshape(-1, cells_z), near_matrix)
    flat, six = shape(cells_x, cells_z), shape(6, cells_x, cells_z)
    mean, variance, first, total = pl.pallas_call(
        far_kernel,
        out_shape=(flat, flat, six, six),
        in_specs=[vmem, vmem, hbm],
        out_specs=(hbm,) * 4,
        scratch_shapes=[
            pltpu.VMEM((128, 128 * GROUP), jnp.bfloat16),
            pltpu.VMEM((256, 128 * GROUP), jnp.float32),
            pltpu.VMEM((DEEP, GROUP, 256, cells_z), jnp.float32),
            pltpu.VMEM(flat.shape, jnp.float32),
            pltpu.VMEM(flat.shape, jnp.float32),
            pltpu.VMEM(six.shape, jnp.float32),
            pltpu.VMEM(six.shape, jnp.float32),
            pltpu.SemaphoreType.DMA((DEEP,)),
            pltpu.SemaphoreType.DMA((16,)),
        ],
        compiler_params=limit(16),
        name="far",
    )(far_received, far_matrix, held(partial))
    return (
        mean.reshape(cells_x, 1, cells_z),
        variance.reshape(cells_x, 1, cells_z),
        first.reshape(6, cells_x, 1, cells_z),
        total.reshape(6, cells_x, 1, cells_z),
    )


def solution(mesh):
    placed = (P("space", None, None), P("space", None, None), P(), P("group", None), P())
    return jax.shard_map(
        local,
        mesh=mesh,
        in_specs=placed,
        out_specs=(
            P(None, ("group", "space"), None),
            P(None, ("group", "space"), None),
            P(None, None, ("group", "space"), None),
            P(None, None, ("group", "space"), None),
        ),
        check_vma=False,
    )
```

```python
import itertools

import jax
import jax.numpy as jnp
import numpy as np
from jax import lax
from jax.experimental import pallas as pl
from jax.experimental.pallas import tpu as pltpu
from jax.sharding import PartitionSpec as P


NEAR_U, NEAR_S, FAR = 5, 3, 4
PAIRS2 = list(itertools.combinations_with_replacement(range(3), 2))
PAIRS3 = list(itertools.combinations_with_replacement(range(3), 3))
FEATURES = 70
WIDE = 64
REST = FEATURES - WIDE
SECTION = WIDE * 8
HIGH = SECTION + 128
TALL = HIGH + SECTION
DEPTH = TALL + HIGH
COLUMNS = SECTION + 128
(ALPHA, KAPPA, HX, HZ, STRENGTH, UP, DOWN, UP2, DOWN2, U0, U0A, U1, UM1, S0, S0A, ONE) = range(16)
PAD = 8
STAGES = 4
GROUP = 4
HELD = 96


def terms():
    word = (KAPPA, HX, HZ)

    def twice(i, j):
        return 2.0 if i != j and i > 0 else 1.0

    def thrice(i, j, k):
        return {1: 1.0, 2: 3.0, 3: 6.0}[len({i, j, k})] if i > 0 else 1.0

    out = [(1.0, U0, ONE, ONE)]
    out += [(1.0, U0A, w, ONE) for w in word]
    out += [(3.0 * twice(i, j), ALPHA, word[i], word[j]) for i, j in PAIRS2]
    out += [(thrice(i, j, k), word[i], word[j], word[k]) for i, j, k in PAIRS3]
    for whole, step in ((U1, UP), (UM1, DOWN)):
        out.append((1.0, whole, ONE, ONE))
        out += [(6.0, step, ALPHA, w) for w in word]
        out += [(3.0 * twice(i, j), step, word[i], word[j]) for i, j in PAIRS2]
    for square in (UP2, DOWN2):
        out.append((3.0, square, ALPHA, ONE))
        out += [(3.0, square, w, ONE) for w in word]
    out.append((1.0, S0, ONE, ONE))
    out += [(1.0, S0A, w, ONE) for w in word]
    out += [(twice(i, j), STRENGTH, word[i], word[j]) for i, j in PAIRS2]
    for step in (UP, DOWN):
        out.append((1.0, S0A, step, ONE))
        out += [(2.0, STRENGTH, step, w) for w in word]
    far = [(1.0, DOWN2, DOWN, ONE), (1.0, UP2, UP, ONE), (1.0, STRENGTH, DOWN2, ONE), (1.0, STRENGTH, UP2, ONE)]
    return out + far


def layout():
    listed = terms()
    factor = np.zeros((1, COLUMNS), np.float32)
    which = np.full((3, COLUMNS), ONE, np.int32)
    for column in range(SECTION + 16 * REST):
        rest = WIDE + (column - SECTION) // 8 % REST
        term = listed[column // 8 if column < SECTION else rest]
        factor[0, column] = term[0]
        which[:, column] = term[1:]
    return factor, which


def pack_kernel(place, owner_there, initial, source, send, padded_u, padded_s, ready, owner, inverse, in_sems, out_sems):
    count = owner.shape[0]
    servers = send.shape[0]
    listed = pltpu.make_async_copy(owner_there, owner, in_sems.at[2 * STAGES])
    listed.start()
    many = 8 // STAGES
    copies = []
    for n in range(STAGES):
        x = pl.ds(many * n, many)
        for k, (there, here) in enumerate(((initial, padded_u), (source, padded_s))):
            inner = here.at[x, pl.ds(PAD, count), :]
            copies.append(pltpu.make_async_copy(there.at[x], inner, in_sems.at[2 * n + k]))
            copies[-1].start()
    for ref in (padded_u, padded_s):
        for x in range(8):
            ref[x, :PAD] = jnp.zeros((PAD, 128), jnp.float32)
            ref[x, PAD + count :] = jnp.zeros((PAD, 128), jnp.float32)
    group = place[0]
    listed.wait()

    def invert(i, carry):
        inverse[owner[i]] = i
        return carry

    lax.fori_loop(0, count, invert, 0, unroll=16)
    first = lax.broadcasted_iota(jnp.int32, (8, 128), 0) < NEAR_U
    sent = []
    for n in range(STAGES):
        copies[2 * n].wait()
        copies[2 * n + 1].wait()

        def fill(s, carry):
            p = inverse[group * servers + s] + PAD
            for x in range(many * n, many * n + many):
                rows_u = padded_u[x, pl.ds(p - NEAR_U // 2, 8), :]
                rows_s = padded_s[x, pl.ds(p - NEAR_S // 2 - NEAR_U, 8), :]
                ready[s, 8 * x : 8 * x + 8, :] = jnp.where(first, rows_u, rows_s)
            return carry

        lax.fori_loop(0, servers, fill, 0, unroll=8)
        here = pl.ds(8 * many * n, 8 * many)
        sent.append(pltpu.make_async_copy(ready.at[:, here], send.at[:, here], out_sems.at[n]))
        sent[-1].start()

    def fill_far(s, carry):
        p = inverse[group * servers + s] + PAD
        for k, (ref, step) in enumerate(((flat_u, -3), (flat_u, 3), (flat_s, -2), (flat_s, 2))):
            ready[s, 64 + 8 * k : 72 + 8 * k, :] = ref[pl.ds(p + step, 8, stride=count + 2 * PAD), :]
        return carry

    flat_u = padded_u.reshape(8 * (count + 2 * PAD), 128)
    flat_s = padded_s.reshape(8 * (count + 2 * PAD), 128)
    lax.fori_loop(0, servers, fill_far, 0, unroll=4)
    here = pl.ds(64, 32)
    sent.append(pltpu.make_async_copy(ready.at[:, here], send.at[:, here], out_sems.at[STAGES]))
    sent[-1].start()
    for copy in sent:
        copy.wait()


def coefficient_kernel(table, pairs, owner, place, factor, which, matrix):
    rows_y = owner.shape[0]

    def find(i, found):
        return jnp.where(owner[i] == place[1], i, found)

    p = lax.fori_loop(0, rows_y, find, 0, unroll=8)
    run = lax.broadcasted_iota(jnp.int32, (64, 128), 0) // 8
    lane = lax.broadcasted_iota(jnp.int32, (64, 128), 1)
    same = lax.broadcasted_iota(jnp.int32, (64, 128), 0) % 8 == lane % 8

    def inside(k):
        return jnp.where(jnp.logical_and(p + k >= 0, p + k < rows_y), 1.0, 0.0)

    ways = inside(1) + inside(-1)
    ways_up = inside(2) + 1.0 + inside(-1)
    ways_down = inside(-2) + 1.0 + inside(1)
    for group in range(4):
        first, second = pairs[group, 0], pairs[group, 1]
        q = []
        for k in range(6):
            swap = jnp.logical_or(run == 1, run == 2 + k)
            q.append(jnp.where(swap, table[second, k], table[first, k]))
        kappa = 0.03 + 0.12 * q[0]
        hx, hy, hz = (-0.5 * (0.3 * q[1 + i] - 0.15) for i in range(3))
        decay = 0.02 + 0.2 * q[4]
        strength = 0.5 + 1.5 * q[5]
        alpha = 1.0 - 6.0 * kappa - decay
        up, down = kappa + hy, kappa - hy
        both = up * down
        values = [None] * ONE
        values[ALPHA], values[KAPPA], values[HX], values[HZ] = alpha, kappa, hx, hz
        values[STRENGTH], values[UP], values[DOWN] = strength, up, down
        values[UP2], values[DOWN2] = up * up, down * down
        values[U0] = alpha * (alpha * alpha + 3.0 * ways * both)
        values[U0A] = 3.0 * (alpha * alpha + ways * both)
        values[U1] = up * (3.0 * alpha * alpha + ways_up * both)
        values[UM1] = down * (3.0 * alpha * alpha + ways_down * both)
        values[S0] = strength * (alpha * alpha + alpha + 1.0 + ways * both)
        values[S0A] = strength * (2.0 * alpha + 1.0)
        rows = slice(64 * group, 64 * group + 64)
        for chunk in range(COLUMNS // 128):
            columns = slice(128 * chunk, 128 * chunk + 128)
            product = jnp.broadcast_to(factor[:, columns], (64, 128))
            for part in range(3):
                index = jnp.broadcast_to(which[part : part + 1, columns], (64, 128))
                chosen = jnp.ones((64, 128), jnp.float32)
                for number, value in enumerate(values):
                    chosen = jnp.where(index == number, value, chosen)
                product = product * chosen
            split = product.reshape(8, 8, 128)
            split = jnp.concatenate([split[:2], split[2:] - split[:1]], axis=0)
            product = jnp.where(same, split.reshape(64, 128), 0.0)
            high = product.astype(jnp.bfloat16)
            low = product - high.astype(jnp.float32)
            if chunk == SECTION // 128:
                low = jnp.where(lane < 8 * REST, 0.0, low)
            else:
                matrix[rows, HIGH + 128 * chunk : HIGH + 128 * chunk + 128] = high
            matrix[rows, columns] = high
            last = TALL + 128 * ((chunk + 1) % (SECTION // 128 + 1))
            matrix[rows, last : last + 128] = low.astype(jnp.bfloat16)


def server_kernel(received, matrix_there, mean, variance, first, total, rows, one, two, phi_a, phi_b, result_a, result_b,
                  mean_out, variance_out, first_out, total_out, matrix, matrix_sem, sems):
    size = mean.shape[0]
    blocks = size // 8
    groups = blocks // GROUP
    lane = lax.broadcasted_iota(jnp.int32, (8, 128), 1)
    brought = pltpu.make_async_copy(matrix_there, matrix, matrix_sem.at[0])
    brought.start()
    zero = jnp.zeros((PAD, 128), jnp.float32)
    for ref, lead in ((rows, (8,)), (one, (3, 8)), (two, (6, 4))):
        for index in itertools.product(*(range(n) for n in lead)):
            ref[index + (slice(0, PAD),)] = zero
            ref[index + (slice(PAD + size, 2 * PAD + size),)] = zero
    for phi in (phi_a, phi_b):
        phi[SECTION + 16 * REST : HIGH, :] = jnp.zeros((128 - 16 * REST, phi.shape[1]), phi.dtype)

    def at(b, step=0):
        return pl.ds(pl.multiple_of(8 * b, 8) + PAD + step, 8)

    def copy(b, carry):
        for k in range(8):
            rows[k, at(b), :] = received[pl.ds(HELD * b + k, 8, stride=8), :]
        return carry

    lax.fori_loop(0, blocks, copy, 0, unroll=4)

    def parts(ref, lead, b):
        c = ref[lead + (at(b), slice(None))]
        east, west = ref[lead + (at(b, 1), slice(None))], ref[lead + (at(b, -1), slice(None))]
        up = jnp.where(lane == 127, 0.0, pltpu.roll(c, 127, 1))
        down = jnp.where(lane == 0, 0.0, pltpu.roll(c, 1, 1))
        return (east + west) + (up + down), east - west, up - down

    def stage1(b, carry):
        for k in range(8):
            for i, value in enumerate(parts(rows, (k,), b)):
                one[i, k, at(b), :] = value
        return carry

    lax.fori_loop(0, 5 * GROUP, stage1, 0, unroll=4)
    inner = (1, 2, 3, 6)

    def stage2(b, carry):
        for n, k in enumerate(inner):
            m, x, z = (parts(one, (i, k), b) for i in range(3))
            words = (m[0], x[0] + m[1], z[0] + m[2], x[1], z[1], z[2])
            for i, value in enumerate(words):
                two[i, n, at(b), :] = value
        return carry

    lax.fori_loop(0, 3 * GROUP, stage2, 0, unroll=4)

    def third(b):
        a = {pair: parts(two, (i, 1), b) for i, pair in enumerate(PAIRS2)}
        out = []
        for i, j, k in PAIRS3:
            if i > 0:
                value = a[(j, k)][i]
            elif j == 0 and k == 0:
                value = a[(0, 0)][0]
            elif j == 0:
                value = a[(0, k)][0] + a[(0, 0)][k]
            elif j == k:
                value = a[(j, j)][0] + a[(0, j)][j]
            else:
                value = 2.0 * a[(j, k)][0] + a[(0, k)][j] + a[(0, j)][k]
            out.append(value)
        return out

    def features(b):
        def words(k, n):
            out = [rows[k, at(b), :]] + [one[i, k, at(b), :] for i in range(3)]
            return out + [two[i, n, at(b), :] for i in range(6)] if n is not None else out

        out = words(2, 1) + third(b)
        out += words(3, 2) + words(1, 0)
        out += words(4, None) + words(0, None)
        out += words(6, 3) + words(7, None) + words(5, None)
        far = HELD * b + 64
        return out + [received[pl.ds(pl.multiple_of(far + 8 * k, 8), 8), :] for k in range(FAR)]

    def fill(group, phi, blocks_of):
        for n in blocks_of:
            columns = slice(128 * n, 128 * n + 128)
            listed = features(GROUP * group + n)
            for i in range(0, FEATURES, 2):
                value = jnp.concatenate([listed[i], listed[i + 1]], axis=0)
                high = value.astype(jnp.bfloat16)
                low = (value - high.astype(jnp.float32)).astype(jnp.bfloat16)
                places = (8 * i, HIGH + 8 * i) if i < WIDE else (8 * i, 8 * (i + REST))
                for place, part in zip(places, (low, high)):
                    phi[place : place + 16, columns] = part

    def multiply(phi, result, blocks_of):
        columns = slice(128 * blocks_of[0], 128 * blocks_of[-1] + 128)
        whole = jnp.dot(matrix[:, :TALL], phi[:, columns], preferred_element_type=jnp.float32)
        rest = jnp.dot(matrix[:, TALL:], phi[SECTION:, columns], preferred_element_type=jnp.float32)
        result[:, columns] = whole + rest

    def add(old, new):
        return new if old is None else old + new

    def reduce(group, result, blocks_of):
        for n in blocks_of:
            columns = slice(128 * n, 128 * n + 128)
            out = pl.ds(pl.multiple_of(8 * (GROUP * group + n), 8), 8)

            def run(number):
                return result[8 * number : 8 * number + 8, columns]

            both = square = None
            firsts, totals = [None] * 6, [None] * 6
            for g in range(4):
                run_a, run_b = run(8 * g), run(8 * g + 1)
                both = add(both, run_a + run_b)
                square = add(square, run_a * run_a + run_b * run_b)
                for i in range(6):
                    gap = run(8 * g + 2 + i)
                    firsts[i] = add(firsts[i], run_b * gap)
                    totals[i] = add(totals[i], gap * gap)
            average = both * 0.125
            mean_out[out, :] = average
            variance_out[out, :] = square * 0.125 - average * average
            for i in range(6):
                first_out[i, out, :] = firsts[i] * 0.25
                total_out[i, out, :] = totals[i] * 0.125

    copies = []

    def finish(part):
        x = pl.ds(part * (size // 4), size // 4)
        for k, (here, there) in enumerate(((mean_out, mean), (variance_out, variance))):
            copies.append(pltpu.make_async_copy(here.at[x, :], there.at[x, :], sems.at[4 * part + k]))
            copies[-1].start()
        for k, (here, there) in enumerate(((first_out, first), (total_out, total))):
            copies.append(pltpu.make_async_copy(here.at[:, x, :], there.at[:, x, :], sems.at[4 * part + 2 + k]))
            copies[-1].start()

    def ahead(group, blocks_of):
        for stage, lead in ((stage2, 3), (stage1, 5)):
            start = GROUP * jnp.minimum(group + lead, groups - 1)
            for n in blocks_of:
                stage(start + n, 0)

    def step(group, now, later):
        for at in range(0, GROUP, 2):
            blocks_of = range(at, at + 2)
            multiply(now[0], now[1], blocks_of)
            fill(jnp.minimum(group + 1, groups - 1), later[0], blocks_of)
            ahead(group, blocks_of)
            reduce(jnp.maximum(group - 1, 0), later[1], blocks_of)

    def body(pair, carry):
        step(2 * pair, (phi_a, result_a), (phi_b, result_b))
        step(2 * pair + 1, (phi_b, result_b), (phi_a, result_a))
        return carry

    fill(0, phi_a, range(GROUP))
    brought.wait()
    many = groups // 8
    for part in range(4):
        lax.fori_loop(part * many, part * many + many, body, 0)
        if part > 0:
            finish(part - 1)
    reduce(groups - 1, result_b, range(GROUP))
    finish(3)
    for copy in copies:
        copy.wait()


def shape(*dims):
    return jax.ShapeDtypeStruct(dims, jnp.float32)


def held(array):
    return pltpu.with_memory_space_constraint(array, pltpu.HBM)


def limit(mib):
    return pltpu.CompilerParams(vmem_limit_bytes=mib * 2**20)


def local(initial, source, table, pairs, owner):
    tile_x, rows_y, cells_z = initial.shape
    servers = lax.axis_size("space")
    group = lax.axis_index("group")
    place = jnp.stack([group, group * servers + lax.axis_index("space")]).astype(jnp.int32)
    all_pairs = lax.all_gather(pairs, "group", axis=0, tiled=True)
    smem = pl.BlockSpec(memory_space=pltpu.SMEM)
    vmem = pl.BlockSpec(memory_space=pltpu.VMEM)
    hbm = pl.BlockSpec(memory_space=pltpu.HBM)
    send = pl.pallas_call(
        pack_kernel,
        out_shape=pltpu.HBM((servers, HELD, cells_z), jnp.float32),
        in_specs=[smem, hbm, hbm, hbm],
        out_specs=hbm,
        scratch_shapes=[
            pltpu.VMEM((8, rows_y + 2 * PAD, cells_z), jnp.float32),
            pltpu.VMEM((8, rows_y + 2 * PAD, cells_z), jnp.float32),
            pltpu.VMEM((servers, HELD, cells_z), jnp.float32),
            pltpu.SMEM((rows_y,), jnp.int32),
            pltpu.SMEM((rows_y,), jnp.int32),
            pltpu.SemaphoreType.DMA((2 * STAGES + 1,)),
            pltpu.SemaphoreType.DMA((STAGES + 1,)),
        ],
        compiler_params=limit(12),
        name="pack",
    )(place, held(owner), held(initial), held(source))
    received = lax.all_to_all(send, "space", split_axis=0, concat_axis=0, tiled=True)
    factor, which = layout()
    matrix = pl.pallas_call(
        coefficient_kernel,
        out_shape=pltpu.HBM((256, DEPTH), jnp.bfloat16),
        in_specs=[smem, smem, smem, smem, vmem, vmem],
        out_specs=vmem,
        compiler_params=limit(8),
        name="coefficients",
    )(table, all_pairs, owner, place, jnp.asarray(factor), jnp.asarray(which))
    cells_x = 8 * servers
    long = cells_x + 2 * PAD
    flat, six = shape(cells_x, cells_z), shape(6, cells_x, cells_z)
    mean, variance, first, total = pl.pallas_call(
        server_kernel,
        out_shape=(flat, flat, six, six),
        in_specs=[vmem, hbm],
        out_specs=(hbm,) * 4,
        scratch_shapes=[
            pltpu.VMEM((8, long, cells_z), jnp.float32),
            pltpu.VMEM((3, 8, long, cells_z), jnp.float32),
            pltpu.VMEM((6, 4, long, cells_z), jnp.float32),
            pltpu.VMEM((TALL, 128 * GROUP), jnp.bfloat16),
            pltpu.VMEM((TALL, 128 * GROUP), jnp.bfloat16),
            pltpu.VMEM((256, 128 * GROUP), jnp.float32),
            pltpu.VMEM((256, 128 * GROUP), jnp.float32),
            pltpu.VMEM(flat.shape, jnp.float32),
            pltpu.VMEM(flat.shape, jnp.float32),
            pltpu.VMEM(six.shape, jnp.float32),
            pltpu.VMEM(six.shape, jnp.float32),
            pltpu.VMEM((256, DEPTH), jnp.bfloat16),
            pltpu.SemaphoreType.DMA((1,)),
            pltpu.SemaphoreType.DMA((16,)),
        ],
        compiler_params=limit(40),
        name="server",
    )(received.reshape(-1, cells_z), held(matrix))
    return (
        mean.reshape(cells_x, 1, cells_z),
        variance.reshape(cells_x, 1, cells_z),
        first.reshape(6, cells_x, 1, cells_z),
        total.reshape(6, cells_x, 1, cells_z),
    )


def solution(mesh):
    placed = (P("space", None, None), P("space", None, None), P(), P("group", None), P())
    return jax.shard_map(
        local,
        mesh=mesh,
        in_specs=placed,
        out_specs=(
            P(None, ("group", "space"), None),
            P(None, ("group", "space"), None),
            P(None, None, ("group", "space"), None),
            P(None, None, ("group", "space"), None),
        ),
        check_vma=False,
    )
```

```python
import itertools

import jax
import jax.numpy as jnp
import numpy as np
from jax import lax
from jax.experimental import pallas as pl
from jax.experimental.pallas import tpu as pltpu
from jax.sharding import PartitionSpec as P


NEAR_U, NEAR_S, FAR = 5, 3, 4
PAIRS2 = list(itertools.combinations_with_replacement(range(3), 2))
PAIRS3 = list(itertools.combinations_with_replacement(range(3), 3))
FEATURES = 70
WIDE = 64
REST = FEATURES - WIDE
SECTION = WIDE * 8
HIGH = SECTION + 128
TALL = HIGH + SECTION
DEPTH = TALL + HIGH
COLUMNS = SECTION + 128
(ALPHA, KAPPA, HX, HZ, STRENGTH, UP, DOWN, UP2, DOWN2, U0, U0A, U1, UM1, S0, S0A, ONE) = range(16)
PAD = 8
STAGES = 4
GROUP = 4
HELD = 96


def terms():
    word = (KAPPA, HX, HZ)

    def twice(i, j):
        return 2.0 if i != j and i > 0 else 1.0

    def thrice(i, j, k):
        return {1: 1.0, 2: 3.0, 3: 6.0}[len({i, j, k})] if i > 0 else 1.0

    out = [(1.0, U0, ONE, ONE)]
    out += [(1.0, U0A, w, ONE) for w in word]
    out += [(3.0 * twice(i, j), ALPHA, word[i], word[j]) for i, j in PAIRS2]
    out += [(thrice(i, j, k), word[i], word[j], word[k]) for i, j, k in PAIRS3]
    for whole, step in ((U1, UP), (UM1, DOWN)):
        out.append((1.0, whole, ONE, ONE))
        out += [(6.0, step, ALPHA, w) for w in word]
        out += [(3.0 * twice(i, j), step, word[i], word[j]) for i, j in PAIRS2]
    for square in (UP2, DOWN2):
        out.append((3.0, square, ALPHA, ONE))
        out += [(3.0, square, w, ONE) for w in word]
    out.append((1.0, S0, ONE, ONE))
    out += [(1.0, S0A, w, ONE) for w in word]
    out += [(twice(i, j), STRENGTH, word[i], word[j]) for i, j in PAIRS2]
    for step in (UP, DOWN):
        out.append((1.0, S0A, step, ONE))
        out += [(2.0, STRENGTH, step, w) for w in word]
    far = [(1.0, DOWN2, DOWN, ONE), (1.0, UP2, UP, ONE), (1.0, STRENGTH, DOWN2, ONE), (1.0, STRENGTH, UP2, ONE)]
    return out + far


def layout():
    listed = terms()
    factor = np.zeros((1, COLUMNS), np.float32)
    which = np.full((3, COLUMNS), ONE, np.int32)
    for column in range(SECTION + 16 * REST):
        rest = WIDE + (column - SECTION) // 8 % REST
        term = listed[column // 8 if column < SECTION else rest]
        factor[0, column] = term[0]
        which[:, column] = term[1:]
    return factor, which


def pack_kernel(place, owner_there, initial, source, send, padded_u, padded_s, ready, owner, inverse, in_sems, out_sems):
    count = owner.shape[0]
    servers = send.shape[0]
    listed = pltpu.make_async_copy(owner_there, owner, in_sems.at[2 * STAGES])
    listed.start()
    many = 8 // STAGES
    copies = []
    for n in range(STAGES):
        x = pl.ds(many * n, many)
        for k, (there, here) in enumerate(((initial, padded_u), (source, padded_s))):
            inner = here.at[x, pl.ds(PAD, count), :]
            copies.append(pltpu.make_async_copy(there.at[x], inner, in_sems.at[2 * n + k]))
            copies[-1].start()
    for ref in (padded_u, padded_s):
        for x in range(8):
            ref[x, :PAD] = jnp.zeros((PAD, 128), jnp.float32)
            ref[x, PAD + count :] = jnp.zeros((PAD, 128), jnp.float32)
    group = place[0]
    listed.wait()

    def invert(i, carry):
        inverse[owner[i]] = i
        return carry

    lax.fori_loop(0, count, invert, 0, unroll=16)
    first = lax.broadcasted_iota(jnp.int32, (8, 128), 0) < NEAR_U
    sent = []
    for n in range(STAGES):
        copies[2 * n].wait()
        copies[2 * n + 1].wait()

        def fill(s, carry):
            p = inverse[group * servers + s] + PAD
            for x in range(many * n, many * n + many):
                rows_u = padded_u[x, pl.ds(p - NEAR_U // 2, 8), :]
                rows_s = padded_s[x, pl.ds(p - NEAR_S // 2 - NEAR_U, 8), :]
                ready[s, 8 * x : 8 * x + 8, :] = jnp.where(first, rows_u, rows_s)
            return carry

        lax.fori_loop(0, servers, fill, 0, unroll=8)
        here = pl.ds(8 * many * n, 8 * many)
        sent.append(pltpu.make_async_copy(ready.at[:, here], send.at[:, here], out_sems.at[n]))
        sent[-1].start()

    def fill_far(s, carry):
        p = inverse[group * servers + s] + PAD
        for k, (ref, step) in enumerate(((flat_u, -3), (flat_u, 3), (flat_s, -2), (flat_s, 2))):
            ready[s, 64 + 8 * k : 72 + 8 * k, :] = ref[pl.ds(p + step, 8, stride=count + 2 * PAD), :]
        return carry

    flat_u = padded_u.reshape(8 * (count + 2 * PAD), 128)
    flat_s = padded_s.reshape(8 * (count + 2 * PAD), 128)
    lax.fori_loop(0, servers, fill_far, 0, unroll=4)
    here = pl.ds(64, 32)
    sent.append(pltpu.make_async_copy(ready.at[:, here], send.at[:, here], out_sems.at[STAGES]))
    sent[-1].start()
    for copy in sent:
        copy.wait()


def coefficient_kernel(table, pairs, owner, place, factor, which, matrix):
    rows_y = owner.shape[0]

    def find(i, found):
        return jnp.where(owner[i] == place[1], i, found)

    p = lax.fori_loop(0, rows_y, find, 0, unroll=8)
    run = lax.broadcasted_iota(jnp.int32, (64, 128), 0) // 8
    lane = lax.broadcasted_iota(jnp.int32, (64, 128), 1)
    same = lax.broadcasted_iota(jnp.int32, (64, 128), 0) % 8 == lane % 8

    def inside(k):
        return jnp.where(jnp.logical_and(p + k >= 0, p + k < rows_y), 1.0, 0.0)

    ways = inside(1) + inside(-1)
    ways_up = inside(2) + 1.0 + inside(-1)
    ways_down = inside(-2) + 1.0 + inside(1)
    bases = []
    for group in range(4):
        first, second = pairs[group, 0], pairs[group, 1]
        q = []
        for k in range(6):
            swap = jnp.logical_or(run == 1, run == 2 + k)
            q.append(jnp.where(swap, table[second, k], table[first, k]))
        kappa = 0.03 + 0.12 * q[0]
        hx, hy, hz = (-0.5 * (0.3 * q[1 + i] - 0.15) for i in range(3))
        decay = 0.02 + 0.2 * q[4]
        strength = 0.5 + 1.5 * q[5]
        alpha = 1.0 - 6.0 * kappa - decay
        up, down = kappa + hy, kappa - hy
        both = up * down
        values = [None] * ONE
        values[ALPHA], values[KAPPA], values[HX], values[HZ] = alpha, kappa, hx, hz
        values[STRENGTH], values[UP], values[DOWN] = strength, up, down
        values[UP2], values[DOWN2] = up * up, down * down
        values[U0] = alpha * (alpha * alpha + 3.0 * ways * both)
        values[U0A] = 3.0 * (alpha * alpha + ways * both)
        values[U1] = up * (3.0 * alpha * alpha + ways_up * both)
        values[UM1] = down * (3.0 * alpha * alpha + ways_down * both)
        values[S0] = strength * (alpha * alpha + alpha + 1.0 + ways * both)
        values[S0A] = strength * (2.0 * alpha + 1.0)
        rows = slice(64 * group, 64 * group + 64)
        for chunk in range(COLUMNS // 128):
            columns = slice(128 * chunk, 128 * chunk + 128)
            product = jnp.broadcast_to(factor[:, columns], (64, 128))
            for part in range(3):
                index = jnp.broadcast_to(which[part : part + 1, columns], (64, 128))
                chosen = jnp.ones((64, 128), jnp.float32)
                for number, value in enumerate(values):
                    chosen = jnp.where(index == number, value, chosen)
                product = product * chosen
            split = product.reshape(8, 8, 128)
            if group == 0:
                bases.append(split[:1])
                near = [split[:1], split[1:2] - split[:1]]
            else:
                near = [split[:2] - bases[chunk]]
            split = jnp.concatenate(near + [split[2:] - split[:1]], axis=0)
            product = jnp.where(same, split.reshape(64, 128), 0.0)
            high = product.astype(jnp.bfloat16)
            low = product - high.astype(jnp.float32)
            if chunk == SECTION // 128:
                low = jnp.where(lane < 8 * REST, 0.0, low)
            else:
                matrix[rows, HIGH + 128 * chunk : HIGH + 128 * chunk + 128] = high
            matrix[rows, columns] = high
            last = TALL + 128 * ((chunk + 1) % (SECTION // 128 + 1))
            matrix[rows, last : last + 128] = low.astype(jnp.bfloat16)


def server_kernel(received, matrix_there, mean, variance, first, total, rows, one, two, phi_a, phi_b, result_a, result_b,
                  mean_out, variance_out, first_out, total_out, matrix, matrix_sem, sems):
    size = mean.shape[0]
    blocks = size // 8
    groups = blocks // GROUP
    lane = lax.broadcasted_iota(jnp.int32, (8, 128), 1)
    brought = pltpu.make_async_copy(matrix_there, matrix, matrix_sem.at[0])
    brought.start()
    zero = jnp.zeros((PAD, 128), jnp.float32)
    for ref, lead in ((rows, (8,)), (one, (3, 8)), (two, (6, 4))):
        for index in itertools.product(*(range(n) for n in lead)):
            ref[index + (slice(0, PAD),)] = zero
            ref[index + (slice(PAD + size, 2 * PAD + size),)] = zero
    for phi in (phi_a, phi_b):
        phi[SECTION + 16 * REST : HIGH, :] = jnp.zeros((128 - 16 * REST, phi.shape[1]), phi.dtype)

    def at(b, step=0):
        return pl.ds(pl.multiple_of(8 * b, 8) + PAD + step, 8)

    def copy(b, carry):
        for k in range(8):
            rows[k, at(b), :] = received[pl.ds(HELD * b + k, 8, stride=8), :]
        return carry

    lax.fori_loop(0, blocks, copy, 0, unroll=4)

    def parts(ref, lead, b):
        c = ref[lead + (at(b), slice(None))]
        east, west = ref[lead + (at(b, 1), slice(None))], ref[lead + (at(b, -1), slice(None))]
        up = jnp.where(lane == 127, 0.0, pltpu.roll(c, 127, 1))
        down = jnp.where(lane == 0, 0.0, pltpu.roll(c, 1, 1))
        return (east + west) + (up + down), east - west, up - down

    def stage1(b, carry):
        for k in range(8):
            for i, value in enumerate(parts(rows, (k,), b)):
                one[i, k, at(b), :] = value
        return carry

    lax.fori_loop(0, 5 * GROUP, stage1, 0, unroll=4)
    inner = (1, 2, 3, 6)

    def stage2(b, carry):
        for n, k in enumerate(inner):
            m, x, z = (parts(one, (i, k), b) for i in range(3))
            words = (m[0], x[0] + m[1], z[0] + m[2], x[1], z[1], z[2])
            for i, value in enumerate(words):
                two[i, n, at(b), :] = value
        return carry

    lax.fori_loop(0, 3 * GROUP, stage2, 0, unroll=4)

    def third(b):
        a = {pair: parts(two, (i, 1), b) for i, pair in enumerate(PAIRS2)}
        out = []
        for i, j, k in PAIRS3:
            if i > 0:
                value = a[(j, k)][i]
            elif j == 0 and k == 0:
                value = a[(0, 0)][0]
            elif j == 0:
                value = a[(0, k)][0] + a[(0, 0)][k]
            elif j == k:
                value = a[(j, j)][0] + a[(0, j)][j]
            else:
                value = 2.0 * a[(j, k)][0] + a[(0, k)][j] + a[(0, j)][k]
            out.append(value)
        return out

    def features(b):
        def words(k, n):
            out = [rows[k, at(b), :]] + [one[i, k, at(b), :] for i in range(3)]
            return out + [two[i, n, at(b), :] for i in range(6)] if n is not None else out

        out = words(2, 1) + third(b)
        out += words(3, 2) + words(1, 0)
        out += words(4, None) + words(0, None)
        out += words(6, 3) + words(7, None) + words(5, None)
        far = HELD * b + 64
        return out + [received[pl.ds(pl.multiple_of(far + 8 * k, 8), 8), :] for k in range(FAR)]

    def fill(group, phi, blocks_of):
        for n in blocks_of:
            columns = slice(128 * n, 128 * n + 128)
            listed = features(GROUP * group + n)
            for i in range(0, FEATURES, 2):
                value = jnp.concatenate([listed[i], listed[i + 1]], axis=0)
                high = value.astype(jnp.bfloat16)
                low = (value - high.astype(jnp.float32)).astype(jnp.bfloat16)
                places = (8 * i, HIGH + 8 * i) if i < WIDE else (8 * i, 8 * (i + REST))
                for place, part in zip(places, (low, high)):
                    phi[place : place + 16, columns] = part

    def multiply(phi, result, blocks_of):
        columns = slice(128 * blocks_of[0], 128 * blocks_of[-1] + 128)
        whole = jnp.dot(matrix[:, :TALL], phi[:, columns], preferred_element_type=jnp.float32)
        rest = jnp.dot(matrix[:, TALL:], phi[SECTION:, columns], preferred_element_type=jnp.float32)
        result[:, columns] = whole + rest

    def add(old, new):
        return new if old is None else old + new

    def reduce(group, result, blocks_of):
        for n in blocks_of:
            columns = slice(128 * n, 128 * n + 128)
            out = pl.ds(pl.multiple_of(8 * (GROUP * group + n), 8), 8)

            def run(number):
                return result[8 * number : 8 * number + 8, columns]

            both = square = None
            firsts, totals = [None] * 6, [None] * 6
            base = run(0)
            for g in range(4):
                run_b = run(8 * g + 1)
                if g > 0:
                    run_a = run(8 * g)
                    both = add(both, run_a)
                    square = add(square, run_a * run_a)
                both = add(both, run_b)
                square = add(square, run_b * run_b)
                run_b = base + run_b
                for i in range(6):
                    gap = run(8 * g + 2 + i)
                    firsts[i] = add(firsts[i], run_b * gap)
                    totals[i] = add(totals[i], gap * gap)
            average = both * 0.125
            mean_out[out, :] = base + average
            variance_out[out, :] = square * 0.125 - average * average
            for i in range(6):
                first_out[i, out, :] = firsts[i] * 0.25
                total_out[i, out, :] = totals[i] * 0.125

    copies = []

    def finish(part):
        x = pl.ds(part * (size // 4), size // 4)
        for k, (here, there) in enumerate(((mean_out, mean), (variance_out, variance))):
            copies.append(pltpu.make_async_copy(here.at[x, :], there.at[x, :], sems.at[4 * part + k]))
            copies[-1].start()
        for k, (here, there) in enumerate(((first_out, first), (total_out, total))):
            copies.append(pltpu.make_async_copy(here.at[:, x, :], there.at[:, x, :], sems.at[4 * part + 2 + k]))
            copies[-1].start()

    def ahead(group, blocks_of):
        for stage, lead in ((stage2, 3), (stage1, 5)):
            start = GROUP * jnp.minimum(group + lead, groups - 1)
            for n in blocks_of:
                stage(start + n, 0)

    def step(group, now, later):
        for at in range(0, GROUP, 2):
            blocks_of = range(at, at + 2)
            multiply(now[0], now[1], blocks_of)
            reduce(jnp.maximum(group - 1, 0), later[1], blocks_of)
            fill(jnp.minimum(group + 1, groups - 1), later[0], blocks_of)
            ahead(group, blocks_of)

    def body(pair, carry):
        step(2 * pair, (phi_a, result_a), (phi_b, result_b))
        step(2 * pair + 1, (phi_b, result_b), (phi_a, result_a))
        return carry

    fill(0, phi_a, range(GROUP))
    brought.wait()
    many = groups // 8
    for part in range(4):
        lax.fori_loop(part * many, part * many + many, body, 0)
        if part > 0:
            finish(part - 1)
    reduce(groups - 1, result_b, range(GROUP))
    finish(3)
    for copy in copies:
        copy.wait()


def shape(*dims):
    return jax.ShapeDtypeStruct(dims, jnp.float32)


def held(array):
    return pltpu.with_memory_space_constraint(array, pltpu.HBM)


def limit(mib):
    return pltpu.CompilerParams(vmem_limit_bytes=mib * 2**20)


def local(initial, source, table, pairs, owner):
    tile_x, rows_y, cells_z = initial.shape
    servers = lax.axis_size("space")
    group = lax.axis_index("group")
    place = jnp.stack([group, group * servers + lax.axis_index("space")]).astype(jnp.int32)
    all_pairs = lax.all_gather(pairs, "group", axis=0, tiled=True)
    smem = pl.BlockSpec(memory_space=pltpu.SMEM)
    vmem = pl.BlockSpec(memory_space=pltpu.VMEM)
    hbm = pl.BlockSpec(memory_space=pltpu.HBM)
    send = pl.pallas_call(
        pack_kernel,
        out_shape=pltpu.HBM((servers, HELD, cells_z), jnp.float32),
        in_specs=[smem, hbm, hbm, hbm],
        out_specs=hbm,
        scratch_shapes=[
            pltpu.VMEM((8, rows_y + 2 * PAD, cells_z), jnp.float32),
            pltpu.VMEM((8, rows_y + 2 * PAD, cells_z), jnp.float32),
            pltpu.VMEM((servers, HELD, cells_z), jnp.float32),
            pltpu.SMEM((rows_y,), jnp.int32),
            pltpu.SMEM((rows_y,), jnp.int32),
            pltpu.SemaphoreType.DMA((2 * STAGES + 1,)),
            pltpu.SemaphoreType.DMA((STAGES + 1,)),
        ],
        compiler_params=limit(12),
        name="pack",
    )(place, held(owner), held(initial), held(source))
    received = lax.all_to_all(send, "space", split_axis=0, concat_axis=0, tiled=True)
    factor, which = layout()
    matrix = pl.pallas_call(
        coefficient_kernel,
        out_shape=pltpu.HBM((256, DEPTH), jnp.bfloat16),
        in_specs=[smem, smem, smem, smem, vmem, vmem],
        out_specs=vmem,
        compiler_params=limit(8),
        name="coefficients",
    )(table, all_pairs, owner, place, jnp.asarray(factor), jnp.asarray(which))
    cells_x = 8 * servers
    long = cells_x + 2 * PAD
    flat, six = shape(cells_x, cells_z), shape(6, cells_x, cells_z)
    mean, variance, first, total = pl.pallas_call(
        server_kernel,
        out_shape=(flat, flat, six, six),
        in_specs=[vmem, hbm],
        out_specs=(hbm,) * 4,
        scratch_shapes=[
            pltpu.VMEM((8, long, cells_z), jnp.float32),
            pltpu.VMEM((3, 8, long, cells_z), jnp.float32),
            pltpu.VMEM((6, 4, long, cells_z), jnp.float32),
            pltpu.VMEM((TALL, 128 * GROUP), jnp.bfloat16),
            pltpu.VMEM((TALL, 128 * GROUP), jnp.bfloat16),
            pltpu.VMEM((256, 128 * GROUP), jnp.float32),
            pltpu.VMEM((256, 128 * GROUP), jnp.float32),
            pltpu.VMEM(flat.shape, jnp.float32),
            pltpu.VMEM(flat.shape, jnp.float32),
            pltpu.VMEM(six.shape, jnp.float32),
            pltpu.VMEM(six.shape, jnp.float32),
            pltpu.VMEM((256, DEPTH), jnp.bfloat16),
            pltpu.SemaphoreType.DMA((1,)),
            pltpu.SemaphoreType.DMA((16,)),
        ],
        compiler_params=limit(40),
        name="server",
    )(received.reshape(-1, cells_z), held(matrix))
    return (
        mean.reshape(cells_x, 1, cells_z),
        variance.reshape(cells_x, 1, cells_z),
        first.reshape(6, cells_x, 1, cells_z),
        total.reshape(6, cells_x, 1, cells_z),
    )


def solution(mesh):
    placed = (P("space", None, None), P("space", None, None), P(), P("group", None), P())
    return jax.shard_map(
        local,
        mesh=mesh,
        in_specs=placed,
        out_specs=(
            P(None, ("group", "space"), None),
            P(None, ("group", "space"), None),
            P(None, None, ("group", "space"), None),
            P(None, None, ("group", "space"), None),
        ),
        check_vma=False,
    )
```

```python
import itertools

import jax
import jax.numpy as jnp
import numpy as np
from jax import lax
from jax.experimental import pallas as pl
from jax.experimental.pallas import tpu as pltpu
from jax.sharding import PartitionSpec as P


NEAR_U, NEAR_S, FAR = 5, 3, 4
PAIRS2 = list(itertools.combinations_with_replacement(range(3), 2))
PAIRS3 = list(itertools.combinations_with_replacement(range(3), 3))
FEATURES = 70
WIDE = 64
REST = FEATURES - WIDE
SECTION = WIDE * 8
HIGH = SECTION + 128
TALL = HIGH + SECTION
DEPTH = TALL + HIGH
COLUMNS = SECTION + 128
(ALPHA, KAPPA, HX, HZ, STRENGTH, UP, DOWN, UP2, DOWN2, U0, U0A, U1, UM1, S0, S0A, ONE) = range(16)
PAD = 8
STAGES = 4
GROUP = 4
HELD = 96


def terms():
    word = (KAPPA, HX, HZ)

    def twice(i, j):
        return 2.0 if i != j and i > 0 else 1.0

    def thrice(i, j, k):
        return {1: 1.0, 2: 3.0, 3: 6.0}[len({i, j, k})] if i > 0 else 1.0

    out = [(1.0, U0, ONE, ONE)]
    out += [(1.0, U0A, w, ONE) for w in word]
    out += [(3.0 * twice(i, j), ALPHA, word[i], word[j]) for i, j in PAIRS2]
    out += [(thrice(i, j, k), word[i], word[j], word[k]) for i, j, k in PAIRS3]
    for whole, step in ((U1, UP), (UM1, DOWN)):
        out.append((1.0, whole, ONE, ONE))
        out += [(6.0, step, ALPHA, w) for w in word]
        out += [(3.0 * twice(i, j), step, word[i], word[j]) for i, j in PAIRS2]
    for square in (UP2, DOWN2):
        out.append((3.0, square, ALPHA, ONE))
        out += [(3.0, square, w, ONE) for w in word]
    out.append((1.0, S0, ONE, ONE))
    out += [(1.0, S0A, w, ONE) for w in word]
    out += [(twice(i, j), STRENGTH, word[i], word[j]) for i, j in PAIRS2]
    for step in (UP, DOWN):
        out.append((1.0, S0A, step, ONE))
        out += [(2.0, STRENGTH, step, w) for w in word]
    far = [(1.0, DOWN2, DOWN, ONE), (1.0, UP2, UP, ONE), (1.0, STRENGTH, DOWN2, ONE), (1.0, STRENGTH, UP2, ONE)]
    return out + far


def layout():
    listed = terms()
    factor = np.zeros((1, COLUMNS), np.float32)
    which = np.full((3, COLUMNS), ONE, np.int32)
    for column in range(SECTION + 16 * REST):
        rest = WIDE + (column - SECTION) // 8 % REST
        term = listed[column // 8 if column < SECTION else rest]
        factor[0, column] = term[0]
        which[:, column] = term[1:]
    return factor, which


def pack_kernel(place, owner_there, initial, source, send, padded_u, padded_s, ready, owner, inverse, in_sems, out_sems):
    count = owner.shape[0]
    servers = send.shape[0]
    listed = pltpu.make_async_copy(owner_there, owner, in_sems.at[2 * STAGES])
    listed.start()
    many = 8 // STAGES
    copies = []
    for n in range(STAGES):
        x = pl.ds(many * n, many)
        for k, (there, here) in enumerate(((initial, padded_u), (source, padded_s))):
            inner = here.at[x, pl.ds(PAD, count), :]
            copies.append(pltpu.make_async_copy(there.at[x], inner, in_sems.at[2 * n + k]))
            copies[-1].start()
    for ref in (padded_u, padded_s):
        for x in range(8):
            ref[x, :PAD] = jnp.zeros((PAD, 128), jnp.float32)
            ref[x, PAD + count :] = jnp.zeros((2 * PAD, 128), jnp.float32)
    group = place[0]
    listed.wait()

    def invert(i, carry):
        inverse[owner[i]] = i
        return carry

    lax.fori_loop(0, count, invert, 0, unroll=16)
    first = lax.broadcasted_iota(jnp.int32, (8, 128), 0) < NEAR_U
    sent = []
    for n in range(STAGES):
        copies[2 * n].wait()
        copies[2 * n + 1].wait()

        def fill(s, carry):
            p = inverse[group * servers + s] + PAD
            for x in range(many * n, many * n + many):
                rows_u = padded_u[x, pl.ds(p - NEAR_U // 2, 8), :]
                rows_s = padded_s[x, pl.ds(p - NEAR_S // 2 - NEAR_U, 8), :]
                ready[s, 8 * x : 8 * x + 8, :] = jnp.where(first, rows_u, rows_s)
            return carry

        lax.fori_loop(0, servers, fill, 0, unroll=8)
        here = pl.ds(8 * many * n, 8 * many)
        sent.append(pltpu.make_async_copy(ready.at[:, here], send.at[:, here], out_sems.at[n]))
        sent[-1].start()

    def fill_far(s, carry):
        p = inverse[group * servers + s] + PAD
        for k, (ref, step) in enumerate(((flat_u, -3), (flat_u, 3), (flat_s, -2), (flat_s, 2))):
            ready[s, 64 + 8 * k : 72 + 8 * k, :] = ref[pl.ds(p + step, 8, stride=count + 3 * PAD), :]
        return carry

    flat_u = padded_u.reshape(8 * (count + 3 * PAD), 128)
    flat_s = padded_s.reshape(8 * (count + 3 * PAD), 128)
    lax.fori_loop(0, servers, fill_far, 0, unroll=4)
    here = pl.ds(64, 32)
    sent.append(pltpu.make_async_copy(ready.at[:, here], send.at[:, here], out_sems.at[STAGES]))
    sent[-1].start()
    for copy in sent:
        copy.wait()


def coefficient_kernel(table, pairs, owner, place, factor, which, matrix):
    rows_y = owner.shape[0]

    def find(i, found):
        return jnp.where(owner[i] == place[1], i, found)

    p = lax.fori_loop(0, rows_y, find, 0, unroll=8)
    run = lax.broadcasted_iota(jnp.int32, (64, 128), 0) // 8
    lane = lax.broadcasted_iota(jnp.int32, (64, 128), 1)
    same = lax.broadcasted_iota(jnp.int32, (64, 128), 0) % 8 == lane % 8

    def inside(k):
        return jnp.where(jnp.logical_and(p + k >= 0, p + k < rows_y), 1.0, 0.0)

    ways = inside(1) + inside(-1)
    ways_up = inside(2) + 1.0 + inside(-1)
    ways_down = inside(-2) + 1.0 + inside(1)
    bases = []
    for group in range(4):
        first, second = pairs[group, 0], pairs[group, 1]
        q = []
        for k in range(6):
            swap = jnp.logical_or(run == 1, run == 2 + k)
            q.append(jnp.where(swap, table[second, k], table[first, k]))
        kappa = 0.03 + 0.12 * q[0]
        hx, hy, hz = (-0.5 * (0.3 * q[1 + i] - 0.15) for i in range(3))
        decay = 0.02 + 0.2 * q[4]
        strength = 0.5 + 1.5 * q[5]
        alpha = 1.0 - 6.0 * kappa - decay
        up, down = kappa + hy, kappa - hy
        both = up * down
        values = [None] * ONE
        values[ALPHA], values[KAPPA], values[HX], values[HZ] = alpha, kappa, hx, hz
        values[STRENGTH], values[UP], values[DOWN] = strength, up, down
        values[UP2], values[DOWN2] = up * up, down * down
        values[U0] = alpha * (alpha * alpha + 3.0 * ways * both)
        values[U0A] = 3.0 * (alpha * alpha + ways * both)
        values[U1] = up * (3.0 * alpha * alpha + ways_up * both)
        values[UM1] = down * (3.0 * alpha * alpha + ways_down * both)
        values[S0] = strength * (alpha * alpha + alpha + 1.0 + ways * both)
        values[S0A] = strength * (2.0 * alpha + 1.0)
        rows = slice(64 * group, 64 * group + 64)
        for chunk in range(COLUMNS // 128):
            columns = slice(128 * chunk, 128 * chunk + 128)
            product = jnp.broadcast_to(factor[:, columns], (64, 128))
            for part in range(3):
                index = jnp.broadcast_to(which[part : part + 1, columns], (64, 128))
                chosen = jnp.ones((64, 128), jnp.float32)
                for number, value in enumerate(values):
                    chosen = jnp.where(index == number, value, chosen)
                product = product * chosen
            split = product.reshape(8, 8, 128)
            if group == 0:
                bases.append(split[:1])
                near = [split[:1], split[1:2] - split[:1]]
            else:
                near = [split[:2] - bases[chunk]]
            split = jnp.concatenate(near + [split[2:] - split[:1]], axis=0)
            product = jnp.where(same, split.reshape(64, 128), 0.0)
            high = product.astype(jnp.bfloat16)
            low = product - high.astype(jnp.float32)
            if chunk == SECTION // 128:
                low = jnp.where(lane < 8 * REST, 0.0, low)
            else:
                matrix[rows, HIGH + 128 * chunk : HIGH + 128 * chunk + 128] = high
            matrix[rows, columns] = high
            last = TALL + 128 * ((chunk + 1) % (SECTION // 128 + 1))
            matrix[rows, last : last + 128] = low.astype(jnp.bfloat16)


def server_kernel(received, matrix_there, mean, variance, first, total, rows, one, two, phi_a, phi_b, result_a, result_b,
                  mean_out, variance_out, first_out, total_out, matrix, matrix_sem, sems):
    size = mean.shape[0]
    blocks = size // 8
    groups = blocks // GROUP
    lane = lax.broadcasted_iota(jnp.int32, (8, 128), 1)
    brought = pltpu.make_async_copy(matrix_there, matrix, matrix_sem.at[0])
    brought.start()
    zero = jnp.zeros((PAD, 128), jnp.float32)
    for ref, lead in ((rows, (8,)), (one, (3, 8)), (two, (6, 4))):
        for index in itertools.product(*(range(n) for n in lead)):
            ref[index + (slice(0, PAD),)] = zero
            ref[index + (slice(PAD + size, 2 * PAD + size),)] = zero
    for phi in (phi_a, phi_b):
        phi[SECTION + 16 * REST : HIGH, :] = jnp.zeros((128 - 16 * REST, phi.shape[1]), phi.dtype)

    def at(b, step=0):
        return pl.ds(pl.multiple_of(8 * b, 8) + PAD + step, 8)

    def copy(b, carry):
        for k in range(8):
            rows[k, at(b), :] = received[pl.ds(HELD * b + k, 8, stride=8), :]
        return carry

    lax.fori_loop(0, blocks, copy, 0, unroll=4)

    def parts(ref, lead, b):
        c = ref[lead + (at(b), slice(None))]
        east, west = ref[lead + (at(b, 1), slice(None))], ref[lead + (at(b, -1), slice(None))]
        up = jnp.where(lane == 127, 0.0, pltpu.roll(c, 127, 1))
        down = jnp.where(lane == 0, 0.0, pltpu.roll(c, 1, 1))
        return (east + west) + (up + down), east - west, up - down

    def stage1(b, carry):
        for k in range(8):
            for i, value in enumerate(parts(rows, (k,), b)):
                one[i, k, at(b), :] = value
        return carry

    lax.fori_loop(0, 5 * GROUP, stage1, 0, unroll=4)
    inner = (1, 2, 3, 6)

    def stage2(b, carry):
        for n, k in enumerate(inner):
            m, x, z = (parts(one, (i, k), b) for i in range(3))
            words = (m[0], x[0] + m[1], z[0] + m[2], x[1], z[1], z[2])
            for i, value in enumerate(words):
                two[i, n, at(b), :] = value
        return carry

    lax.fori_loop(0, 3 * GROUP, stage2, 0, unroll=4)

    def third(b):
        a = {pair: parts(two, (i, 1), b) for i, pair in enumerate(PAIRS2)}
        out = []
        for i, j, k in PAIRS3:
            if i > 0:
                value = a[(j, k)][i]
            elif j == 0 and k == 0:
                value = a[(0, 0)][0]
            elif j == 0:
                value = a[(0, k)][0] + a[(0, 0)][k]
            elif j == k:
                value = a[(j, j)][0] + a[(0, j)][j]
            else:
                value = 2.0 * a[(j, k)][0] + a[(0, k)][j] + a[(0, j)][k]
            out.append(value)
        return out

    def features(b):
        def words(k, n):
            out = [rows[k, at(b), :]] + [one[i, k, at(b), :] for i in range(3)]
            return out + [two[i, n, at(b), :] for i in range(6)] if n is not None else out

        out = words(2, 1) + third(b)
        out += words(3, 2) + words(1, 0)
        out += words(4, None) + words(0, None)
        out += words(6, 3) + words(7, None) + words(5, None)
        far = HELD * b + 64
        return out + [received[pl.ds(pl.multiple_of(far + 8 * k, 8), 8), :] for k in range(FAR)]

    def fill(group, phi, blocks_of):
        for n in blocks_of:
            columns = slice(128 * n, 128 * n + 128)
            listed = features(GROUP * group + n)
            for i in range(0, FEATURES, 2):
                value = jnp.concatenate([listed[i], listed[i + 1]], axis=0)
                high = value.astype(jnp.bfloat16)
                low = (value - high.astype(jnp.float32)).astype(jnp.bfloat16)
                places = (8 * i, HIGH + 8 * i) if i < WIDE else (8 * i, 8 * (i + REST))
                for place, part in zip(places, (low, high)):
                    phi[place : place + 16, columns] = part

    def multiply(phi, result, blocks_of):
        columns = slice(128 * blocks_of[0], 128 * blocks_of[-1] + 128)
        whole = jnp.dot(matrix[:, :TALL], phi[:, columns], preferred_element_type=jnp.float32)
        rest = jnp.dot(matrix[:, TALL:], phi[SECTION:, columns], preferred_element_type=jnp.float32)
        result[:, columns] = whole + rest

    def add(old, new):
        return new if old is None else old + new

    def reduce(group, result, blocks_of):
        for n in blocks_of:
            columns = slice(128 * n, 128 * n + 128)
            out = pl.ds(pl.multiple_of(8 * (GROUP * group + n), 8), 8)

            def run(number):
                return result[8 * number : 8 * number + 8, columns]

            both = square = None
            firsts, totals = [None] * 6, [None] * 6
            base = run(0)
            for g in range(4):
                run_b = run(8 * g + 1)
                if g > 0:
                    run_a = run(8 * g)
                    both = add(both, run_a)
                    square = add(square, run_a * run_a)
                both = add(both, run_b)
                square = add(square, run_b * run_b)
                run_b = base + run_b
                for i in range(6):
                    gap = run(8 * g + 2 + i)
                    firsts[i] = add(firsts[i], run_b * gap)
                    totals[i] = add(totals[i], gap * gap)
            average = both * 0.125
            mean_out[out, :] = base + average
            variance_out[out, :] = square * 0.125 - average * average
            for i in range(6):
                first_out[i, out, :] = firsts[i] * 0.25
                total_out[i, out, :] = totals[i] * 0.125

    copies = []

    def finish(part):
        x = pl.ds(part * (size // 4), size // 4)
        for k, (here, there) in enumerate(((mean_out, mean), (variance_out, variance))):
            copies.append(pltpu.make_async_copy(here.at[x, :], there.at[x, :], sems.at[4 * part + k]))
            copies[-1].start()
        for k, (here, there) in enumerate(((first_out, first), (total_out, total))):
            copies.append(pltpu.make_async_copy(here.at[:, x, :], there.at[:, x, :], sems.at[4 * part + 2 + k]))
            copies[-1].start()

    def ahead(group, blocks_of):
        for stage, lead in ((stage2, 3), (stage1, 5)):
            start = GROUP * jnp.minimum(group + lead, groups - 1)
            for n in blocks_of:
                stage(start + n, 0)

    def step(group, now, later):
        for at in range(0, GROUP, 2):
            blocks_of = range(at, at + 2)
            multiply(now[0], now[1], blocks_of)
            reduce(jnp.maximum(group - 1, 0), later[1], blocks_of)
            fill(jnp.minimum(group + 1, groups - 1), later[0], blocks_of)
            ahead(group, blocks_of)

    def body(pair, carry):
        step(2 * pair, (phi_a, result_a), (phi_b, result_b))
        step(2 * pair + 1, (phi_b, result_b), (phi_a, result_a))
        return carry

    fill(0, phi_a, range(GROUP))
    brought.wait()
    many = groups // 8
    for part in range(4):
        lax.fori_loop(part * many, part * many + many, body, 0)
        if part > 0:
            finish(part - 1)
    reduce(groups - 1, result_b, range(GROUP))
    finish(3)
    for copy in copies:
        copy.wait()


def shape(*dims):
    return jax.ShapeDtypeStruct(dims, jnp.float32)


def held(array):
    return pltpu.with_memory_space_constraint(array, pltpu.HBM)


def limit(mib):
    return pltpu.CompilerParams(vmem_limit_bytes=mib * 2**20)


def local(initial, source, table, pairs, owner):
    tile_x, rows_y, cells_z = initial.shape
    servers = lax.axis_size("space")
    group = lax.axis_index("group")
    place = jnp.stack([group, group * servers + lax.axis_index("space")]).astype(jnp.int32)
    all_pairs = lax.all_gather(pairs, "group", axis=0, tiled=True)
    smem = pl.BlockSpec(memory_space=pltpu.SMEM)
    vmem = pl.BlockSpec(memory_space=pltpu.VMEM)
    hbm = pl.BlockSpec(memory_space=pltpu.HBM)
    send = pl.pallas_call(
        pack_kernel,
        out_shape=pltpu.HBM((servers, HELD, cells_z), jnp.float32),
        in_specs=[smem, hbm, hbm, hbm],
        out_specs=hbm,
        scratch_shapes=[
            pltpu.VMEM((8, rows_y + 3 * PAD, cells_z), jnp.float32),
            pltpu.VMEM((8, rows_y + 3 * PAD, cells_z), jnp.float32),
            pltpu.VMEM((servers, HELD, cells_z), jnp.float32),
            pltpu.SMEM((rows_y,), jnp.int32),
            pltpu.SMEM((rows_y,), jnp.int32),
            pltpu.SemaphoreType.DMA((2 * STAGES + 1,)),
            pltpu.SemaphoreType.DMA((STAGES + 1,)),
        ],
        compiler_params=limit(12),
        name="pack",
    )(place, held(owner), held(initial), held(source))
    received = lax.all_to_all(send, "space", split_axis=0, concat_axis=0, tiled=True)
    factor, which = layout()
    matrix = pl.pallas_call(
        coefficient_kernel,
        out_shape=pltpu.HBM((256, DEPTH), jnp.bfloat16),
        in_specs=[smem, smem, smem, smem, vmem, vmem],
        out_specs=vmem,
        compiler_params=limit(8),
        name="coefficients",
    )(table, all_pairs, owner, place, jnp.asarray(factor), jnp.asarray(which))
    cells_x = 8 * servers
    long = cells_x + 2 * PAD
    flat, six = shape(cells_x, cells_z), shape(6, cells_x, cells_z)
    mean, variance, first, total = pl.pallas_call(
        server_kernel,
        out_shape=(flat, flat, six, six),
        in_specs=[vmem, hbm],
        out_specs=(hbm,) * 4,
        scratch_shapes=[
            pltpu.VMEM((8, long, cells_z), jnp.float32),
            pltpu.VMEM((3, 8, long, cells_z), jnp.float32),
            pltpu.VMEM((6, 4, long, cells_z), jnp.float32),
            pltpu.VMEM((TALL, 128 * GROUP), jnp.bfloat16),
            pltpu.VMEM((TALL, 128 * GROUP), jnp.bfloat16),
            pltpu.VMEM((256, 128 * GROUP), jnp.float32),
            pltpu.VMEM((256, 128 * GROUP), jnp.float32),
            pltpu.VMEM(flat.shape, jnp.float32),
            pltpu.VMEM(flat.shape, jnp.float32),
            pltpu.VMEM(six.shape, jnp.float32),
            pltpu.VMEM(six.shape, jnp.float32),
            pltpu.VMEM((256, DEPTH), jnp.bfloat16),
            pltpu.SemaphoreType.DMA((1,)),
            pltpu.SemaphoreType.DMA((16,)),
        ],
        compiler_params=limit(40),
        name="server",
    )(received.reshape(-1, cells_z), held(matrix))
    return (
        mean.reshape(cells_x, 1, cells_z),
        variance.reshape(cells_x, 1, cells_z),
        first.reshape(6, cells_x, 1, cells_z),
        total.reshape(6, cells_x, 1, cells_z),
    )


def solution(mesh):
    placed = (P("space", None, None), P("space", None, None), P(), P("group", None), P())
    return jax.shard_map(
        local,
        mesh=mesh,
        in_specs=placed,
        out_specs=(
            P(None, ("group", "space"), None),
            P(None, ("group", "space"), None),
            P(None, None, ("group", "space"), None),
            P(None, None, ("group", "space"), None),
        ),
        check_vma=False,
    )
```
